128 devices in a mesh: row: 16 (over y, z_lo, core), col: 8 (over z_hi, x).
Axes of the slice: x: 4, y: 4, z: 4 (z_hi: 2, z_lo: 2; z = z_hi * 2 + z_lo), core: 2. Of those that a mesh axis runs over, the one named last changes fastest.
Arguments:
- points: float32 [49152, 16], P(('row', 'col')), may hold values from -6 to 6
- targets: float32 [49152, 16], P(('row', 'col')), may hold values from -6 to 6
- initial: float32 [49152, 16], P(('row', 'col')), may hold values from -3 to 3
- lengthscale: float32 [16], replicated, may hold values from 2 to 8
Outputs:
- solution: float32 [49152, 16], P(('row', 'col'))
- residual: float32 [49152, 16], P(('row', 'col'))
The draws below stay inside these ranges and needn't reach their ends.
All inputs are finite; a program needn't handle non-finite values.
Results may differ from the reference program's by a relative error of at most 0.0003.
Values sent between devices are 32-bit elements; how exact they have to be, the bound alone decides.
A program may use at most 64 MiB of HBM per device.

```python
import math
import jax
import jax.numpy as jnp
from jax import lax

FEAT = 16
VECS = 16
ITERS = 2
POINTS = 49152


def levels(own_key, shape, cuts, low, high):
    def one(position, blocks):
        steps = jax.random.uniform(jax.random.fold_in(jax.random.fold_in(own_key, 6), position), (blocks,), jnp.float32, low / len(cuts), high / len(cuts))
        return jnp.repeat(jnp.exp(steps), shape[position] // blocks).reshape((-1,) + (1,) * (len(shape) - position - 1))

    gain = one(*cuts[0])
    for cut in cuts[1:]:
        gain = gain * one(*cut)
    return gain


def centred(rng, dims, width, reach, shards=(), held_as=jnp.bfloat16):
    values = width * jax.random.normal(rng, dims, jnp.float32)
    if shards:
        values = values * levels(rng, dims, shards, -0.22, 0.18)
    return jnp.clip(values, -reach, reach).astype(held_as)


def setup_inputs(seed: int = 0) -> dict:
    arg_keys = jax.random.split(jax.random.key(seed), 5)
    points = centred(arg_keys[0], (POINTS, FEAT), 1.0, 6.0, ((0, 128),), jnp.float32)
    targets = centred(arg_keys[1], (POINTS, VECS), 1.0, 6.0, ((0, 128),), jnp.float32)
    initial = centred(arg_keys[2], (POINTS, VECS), 0.5, 3.0, ((0, 128),), jnp.float32)
    lengthscale = jnp.clip(jnp.exp(jax.random.uniform(arg_keys[3], (FEAT,), jnp.float32, math.log(2.0), math.log(8.0))), 2.0, 8.0)
    return {"points": points, "targets": targets, "initial": initial, "lengthscale": lengthscale}


ROOT_FIVE = 5.0 ** 0.5
NOISE_VAR = 0.5

def matern_apply(left_pts, left_sq, right_pts, right_sq, vectors):
    crossed = jnp.dot(left_pts, right_pts.T, precision=lax.Precision.HIGHEST)
    squared = jnp.maximum(left_sq[:, None] + right_sq[None, :] - 2.0 * crossed, 0.0)
    distance = jnp.sqrt(squared)
    kernel = (1.0 + ROOT_FIVE * distance + 5.0 / 3.0 * squared) * jnp.exp(-ROOT_FIVE * distance)
    return jnp.dot(kernel, vectors, precision=lax.Precision.HIGHEST)

def reference(points, targets, initial, lengthscale):
    scaled = points / lengthscale[None, :]
    squares = lax.optimization_barrier(jnp.sum(scaled * scaled, axis=1))
    blocksize = 512 if POINTS % 512 == 0 else POINTS
    nblocks = POINTS // blocksize

    def operate(vectors):

        def one_block(pair):
            return matern_apply(pair[0], pair[1], scaled, squares, vectors)
        parts = lax.map(one_block, (scaled.reshape(nblocks, blocksize, FEAT), squares.reshape(nblocks, blocksize)))
        return parts.reshape(POINTS, VECS) + NOISE_VAR * vectors
    solution = initial
    residual = targets - operate(initial)
    direction = residual
    norm_now = lax.optimization_barrier(jnp.sum(residual * residual, axis=0))
    for number in range(ITERS):
        image = operate(direction)
        step_size = norm_now / lax.optimization_barrier(jnp.sum(direction * image, axis=0))
        solution = solution + step_size[None, :] * direction
        residual = residual - step_size[None, :] * image
        norm_next = lax.optimization_barrier(jnp.sum(residual * residual, axis=0))
        direction = residual + (norm_next / norm_now)[None, :] * direction
        norm_now = norm_next
    return (solution, residual)
```

```python
import math

import jax
import jax.numpy as jnp
from jax import lax
from jax.experimental import pallas as pl
from jax.experimental.pallas import tpu as pltpu
from jax.sharding import PartitionSpec as P

MESH = pl.DeviceIdType.MESH
F32, BF16 = jnp.float32, jnp.bfloat16
NOISE_VAR = 0.5
LN2 = math.log(2.0)
DIST_SCALE = math.sqrt(5.0) / LN2
VECS = 16
DEPTH = 128
CHUNK = 768
PIECE = 1024
SUB = 256
KEPT = 1


def split3(x):
    first = x.astype(BF16)
    rest = x - first.astype(F32)
    second = rest.astype(BF16)
    third = (rest - second.astype(F32)).astype(BF16)
    return first, second, third


def stacked(z, left):
    a, b, c = split3(z)
    qa, qb, qc = split3(jnp.sum(z * z, axis=0, keepdims=True))
    row = lax.broadcasted_iota(jnp.int32, z.shape, 0)
    base = 0 if left else 3
    tail = jnp.where(row == base, qa.astype(F32), 0.0)
    tail = jnp.where(row == base + 1, qb.astype(F32), tail)
    tail = jnp.where(row == base + 2, qc.astype(F32), tail)
    other = 3 - base
    tail = jnp.where((row >= other) & (row < other + 3), 1.0, tail)
    a, b, c = a.astype(F32), b.astype(F32), c.astype(F32)
    zero = jnp.zeros_like(tail)
    if left:
        return jnp.concatenate([a, a, b, b, a, c, tail, zero], axis=0)
    a, b, c = -2.0 * a, -2.0 * b, -2.0 * c
    return jnp.concatenate([a, b, a, b, c, a, tail, zero], axis=0)


def matern(s):
    s = jnp.maximum(s, 1e-30)
    dist = s * lax.rsqrt(s)
    shifted = dist + 1.5 / LN2
    return (shifted * shifted + 0.75 / LN2**2) * jnp.exp2(math.log2(LN2**2 / 3.0) - dist)


def make_kernel(rows_n, cols_n, own):
    span = rows_n * own
    wide = cols_n * own
    n_chunks = wide // CHUNK
    n_pieces = span // PIECE
    per_chunk = CHUNK // own
    slots = 3

    def kernel(
        pts_ref, init_ref, targ_ref, scale_ref,
        sol_ref, res_ref, low_hbm,
        high, low, stage, left, right, vecs, first_own, first_all, right_all,
        vec_own, vec_all, part, part_all, dot_a, dot_a_all, dot_b, dot_b_all,
        col_send, col_recv, row_send, row_recv, stage_sem,
    ):
        my_row, my_col = lax.axis_index("row"), lax.axis_index("col")

        barrier = pltpu.get_barrier_semaphore()

        @pl.loop(1, rows_n)
        def _(k):
            pl.semaphore_signal(
                barrier, inc=1, device_id=(lax.rem(my_row + k, rows_n), my_col), device_id_type=MESH
            )

        @pl.loop(1, cols_n)
        def _(k):
            pl.semaphore_signal(
                barrier, inc=1, device_id=(my_row, lax.rem(my_col + k, cols_n)), device_id_type=MESH
            )

        pl.semaphore_wait(barrier, rows_n - 1 + cols_n - 1)

        def to_rows(phase, src, dst, k):
            return pltpu.make_async_remote_copy(
                src_ref=src, dst_ref=dst.at[my_row],
                send_sem=row_send.at[phase, k], recv_sem=row_recv.at[phase, k],
                device_id=(lax.rem(my_row + k, rows_n), my_col), device_id_type=MESH,
            )

        def to_cols(phase, src, dst, k):
            return pltpu.make_async_remote_copy(
                src_ref=src, dst_ref=dst.at[my_col],
                send_sem=col_send.at[phase, k], recv_sem=col_recv.at[phase, k],
                device_id=(my_row, lax.rem(my_col + k, cols_n)), device_id_type=MESH,
            )

        def start_all(make, phase, src, dst, count):
            @pl.loop(1, count)
            def _(k):
                make(phase, src, dst, k).start()

        def wait_all(make, phase, src, dst, count):
            @pl.loop(1, count)
            def _(k):
                make(phase, src, dst, k).wait()

        z_own = pts_ref[...] / scale_ref[...] * DIST_SCALE
        first_own[0:VECS, :] = z_own
        first_own[VECS:, :] = init_ref[...]
        points_own = first_own.at[pl.ds(0, VECS)]
        start_all(to_cols, 0, points_own, right_all, cols_n)
        start_all(to_rows, 0, first_own, first_all, rows_n)
        first_all[my_row] = first_own[...]
        right_all[my_col] = z_own
        wait_all(to_cols, 0, points_own, right_all, cols_n)
        for slot in range(cols_n):
            right[:, slot * own:(slot + 1) * own] = stacked(right_all[slot], False).astype(BF16)
        wait_all(to_rows, 0, first_own, first_all, rows_n)

        def put_vecs(slot, block):
            here = pl.ds(pl.multiple_of(slot * own, 128), own)
            a, b, c = split3(block)
            vecs[0:VECS, here] = a
            vecs[VECS:2 * VECS, here] = b
            vecs[2 * VECS:, here] = c

        @pl.loop(0, rows_n)
        def _(slot):
            here = pl.ds(pl.multiple_of(slot * own, 128), own)
            left[here, :] = stacked(first_all[slot, 0:VECS], True).T.astype(BF16)
            put_vecs(slot, first_all[slot, VECS:])

        def fold(acc, acc_low):
            return acc[0:VECS] + acc[VECS:2 * VECS] + acc[2 * VECS:] + acc_low

        def send_part(call, chunk, total):
            for n in range(per_chunk):
                owner = chunk * per_chunk + n
                part[call, owner] = total[:, n * own:(n + 1) * own]

                @pl.when(owner != my_col)
                def _():
                    part_copy(call, owner).start()

        def part_copy(call, owner):
            k = lax.rem(owner - my_col + cols_n, cols_n)
            return to_cols(1 + call, part.at[call, owner], part_all.at[call], k)

        def reduced(call, block):
            @pl.loop(1, cols_n)
            def _(k):
                part_copy(call, lax.rem(my_col + k, cols_n)).wait()
            part_all[call, my_col] = part[call, my_col]
            total = part_all[call, 0]
            for slot in range(1, cols_n):
                total = total + part_all[call, slot]
            return total + NOISE_VAR * block

        def low_copy(chunk, piece, slot, out):
            away = low_hbm.at[chunk - KEPT, piece]
            here = stage.at[slot]
            if out:
                return pltpu.make_async_copy(here, away, stage_sem.at[slot])
            return pltpu.make_async_copy(away, here, stage_sem.at[slot])

        for chunk in range(n_chunks):
            cols = slice(chunk * CHUNK, (chunk + 1) * CHUNK)

            def make_piece(piece, carry, chunk=chunk, cols=cols):
                acc, acc_low = carry
                if chunk >= KEPT:
                    count = (chunk - KEPT) * n_pieces + piece
                    slot = lax.rem(count, slots)

                    @pl.when(count >= slots)
                    def _():
                        low_copy(chunk, piece, slot, True).wait()
                for sub in range(PIECE // SUB):
                    rows = pl.ds(pl.multiple_of(piece * PIECE + sub * SUB, SUB), SUB)
                    m = matern(jnp.dot(left[rows, :], right[:, cols], preferred_element_type=F32))
                    h = m.astype(BF16)
                    l = (m - h.astype(F32)).astype(BF16)
                    high[rows, cols] = h
                    if chunk < KEPT:
                        low[rows, cols] = l
                    else:
                        stage[slot, sub * SUB:(sub + 1) * SUB, :] = l
                    acc = acc + jnp.dot(vecs[:, rows], h, preferred_element_type=F32)
                    acc_low = acc_low + jnp.dot(vecs[0:VECS, rows], l, preferred_element_type=F32)
                if chunk >= KEPT:
                    low_copy(chunk, piece, slot, True).start()
                return acc, acc_low

            acc, acc_low = lax.fori_loop(
                0, n_pieces, make_piece,
                (jnp.zeros((3 * VECS, CHUNK), F32), jnp.zeros((VECS, CHUNK), F32)),
            )
            send_part(0, chunk, fold(acc, acc_low))

        total_pieces = (n_chunks - KEPT) * n_pieces
        for slot in range(slots):
            low_copy(KEPT, 0, slot, True).wait()

        def prefetch(count):
            low_copy(KEPT + count // n_pieces, lax.rem(count, n_pieces), lax.rem(count, slots), False).start()

        def apply(call):
            for chunk in range(n_chunks):
                cols = slice(chunk * CHUNK, (chunk + 1) * CHUNK)
                if chunk < KEPT:
                    acc = jnp.dot(vecs[...], high[:, cols], preferred_element_type=F32)
                    acc_low = jnp.dot(vecs[0:VECS, :], low[:, cols], preferred_element_type=F32)
                else:
                    def use_piece(piece, carry, chunk=chunk, cols=cols):
                        acc, acc_low = carry
                        rows = pl.ds(pl.multiple_of(piece * PIECE, PIECE), PIECE)
                        acc = acc + jnp.dot(vecs[:, rows], high[rows, cols], preferred_element_type=F32)
                        count = (chunk - KEPT) * n_pieces + piece
                        slot = lax.rem(count, slots)
                        low_copy(chunk, piece, slot, False).wait()
                        acc_low = acc_low + jnp.dot(
                            vecs[0:VECS, rows], stage[slot], preferred_element_type=F32
                        )

                        @pl.when(count + slots < total_pieces)
                        def _():
                            prefetch(count + slots)
                        return acc, acc_low

                    acc, acc_low = lax.fori_loop(
                        0, n_pieces, use_piece,
                        (jnp.zeros((3 * VECS, CHUNK), F32), jnp.zeros((VECS, CHUNK), F32)),
                    )
                send_part(call, chunk, fold(acc, acc_low))

        def spread(phase, block):
            vec_own[phase] = block
            start_all(to_rows, 1 + phase, vec_own.at[phase], vec_all.at[phase], rows_n)
            vec_all[phase, my_row] = block
            wait_all(to_rows, 1 + phase, vec_own.at[phase], vec_all.at[phase], rows_n)

            @pl.loop(0, rows_n)
            def _(slot):
                put_vecs(slot, vec_all[phase, slot])

        def lanes(x):
            total = x[:, 0:128]
            for n in range(1, own // 128):
                total = total + x[:, n * 128:(n + 1) * 128]
            return total

        def dots(phase, pairs):
            size = VECS * len(pairs)
            for n, (x, y) in enumerate(pairs):
                dot_a[phase, n * VECS:(n + 1) * VECS, :] = lanes(x * y)
            used = pl.ds(0, size)
            mine = dot_a.at[phase, used]
            theirs = dot_a_all.at[phase, :, used]
            start_all(to_cols, 4 + phase, mine, theirs, cols_n)
            dot_a_all[phase, my_col, 0:size] = dot_a[phase, 0:size]
            wait_all(to_cols, 4 + phase, mine, theirs, cols_n)
            total = dot_a_all[phase, 0, 0:size]
            for slot in range(1, cols_n):
                total = total + dot_a_all[phase, slot, 0:size]
            dot_b[phase, 0:size] = total
            mine = dot_b.at[phase, used]
            theirs = dot_b_all.at[phase, :, used]
            start_all(to_rows, 3 + phase, mine, theirs, rows_n)
            dot_b_all[phase, my_row, 0:size] = total
            wait_all(to_rows, 3 + phase, mine, theirs, rows_n)
            total = dot_b_all[phase, 0, 0:size]
            for slot in range(1, rows_n):
                total = total + dot_b_all[phase, slot, 0:size]
            total = jnp.sum(total, axis=1, keepdims=True)
            return [total[n * VECS:(n + 1) * VECS] for n in range(len(pairs))]

        for count in range(slots):
            prefetch(count)
        init = init_ref[...]
        res0 = targ_ref[...] - reduced(0, init)
        spread(0, res0)
        apply(1)
        for count in range(slots):
            prefetch(count)
        image0 = reduced(1, res0)
        norm0, curve0 = dots(0, [(res0, res0), (res0, image0)])
        alpha0 = norm0 / curve0
        res1 = res0 - alpha0 * image0
        spread(1, res1)
        apply(2)
        half = reduced(2, res1)
        norm1, own_curve, cross = dots(1, [(res1, res1), (res1, half), (res1 + res1, image0)])
        beta0 = norm1 / norm0
        curve1 = own_curve + beta0 * cross + beta0 * beta0 * curve0
        alpha1 = norm1 / curve1
        sol_ref[...] = init + alpha0 * res0 + alpha1 * (res1 + beta0 * res0)
        res_ref[...] = res1 - alpha1 * (half + beta0 * image0)

    def scratch():
        return [
            pltpu.VMEM((span, wide), BF16),
            pltpu.VMEM((span, KEPT * CHUNK), BF16),
            pltpu.VMEM((slots, PIECE, CHUNK), BF16),
            pltpu.VMEM((span, DEPTH), BF16),
            pltpu.VMEM((DEPTH, wide), BF16),
            pltpu.VMEM((3 * VECS, span), BF16),
            pltpu.VMEM((2 * VECS, own), F32),
            pltpu.VMEM((rows_n, 2 * VECS, own), F32),
            pltpu.VMEM((cols_n, VECS, own), F32),
            pltpu.VMEM((2, VECS, own), F32),
            pltpu.VMEM((2, rows_n, VECS, own), F32),
            pltpu.VMEM((3, cols_n, VECS, own), F32),
            pltpu.VMEM((3, cols_n, VECS, own), F32),
            pltpu.VMEM((2, 3 * VECS, 128), F32),
            pltpu.VMEM((2, cols_n, 3 * VECS, 128), F32),
            pltpu.VMEM((2, 3 * VECS, 128), F32),
            pltpu.VMEM((2, rows_n, 3 * VECS, 128), F32),
            pltpu.SemaphoreType.DMA((6, cols_n)),
            pltpu.SemaphoreType.DMA((6, cols_n)),
            pltpu.SemaphoreType.DMA((5, rows_n)),
            pltpu.SemaphoreType.DMA((5, rows_n)),
            pltpu.SemaphoreType.DMA((slots,)),
        ]

    vmem = pl.BlockSpec(memory_space=pltpu.VMEM)
    return pl.pallas_call(
        kernel,
        out_shape=[
            jax.ShapeDtypeStruct((VECS, own), F32),
            jax.ShapeDtypeStruct((VECS, own), F32),
            jax.ShapeDtypeStruct((n_chunks - KEPT, n_pieces, PIECE, CHUNK), BF16),
        ],
        in_specs=[vmem] * 4,
        out_specs=[vmem, vmem, pl.BlockSpec(memory_space=pl.ANY)],
        scratch_shapes=scratch(),
        compiler_params=pltpu.CompilerParams(
            collective_id=0, has_side_effects=True, vmem_limit_bytes=60 * 2**20
        ),
        name="conjugate_gradients",
    )


def solution(mesh):
    rows_n, cols_n = mesh.shape["row"], mesh.shape["col"]

    def shards(points, targets, initial, lengthscale):
        call = make_kernel(rows_n, cols_n, points.shape[0])
        sol, res, _ = call(points.T, initial.T, targets.T, lengthscale[:, None])
        return sol.T, res.T

    spec = P(("row", "col"), None)
    return jax.shard_map(
        shards, mesh=mesh, in_specs=(spec, spec, spec, P()), out_specs=(spec, spec), check_vma=False
    )
```

```python
import math

import jax
import jax.numpy as jnp
from jax import lax
from jax.experimental import pallas as pl
from jax.experimental.pallas import tpu as pltpu
from jax.sharding import PartitionSpec as P

MESH = pl.DeviceIdType.MESH
F32, BF16 = jnp.float32, jnp.bfloat16
NOISE_VAR = 0.5
LN2 = math.log(2.0)
DIST_SCALE = math.sqrt(5.0) / LN2
VECS = 16
DEPTH = 128
CHUNK = 768
PIECE = 768
SUB = 256
STAGES = 3
EARLY = 3
LAG = 8


def split3(x):
    first = x.astype(BF16)
    rest = x - first.astype(F32)
    second = rest.astype(BF16)
    third = (rest - second.astype(F32)).astype(BF16)
    return first, second, third


def stacked(z, left):
    a, b, c = split3(z)
    qa, qb, qc = split3(jnp.sum(z * z, axis=0, keepdims=True))
    row = lax.broadcasted_iota(jnp.int32, z.shape, 0)
    base = 0 if left else 3
    tail = jnp.where(row == base, qa.astype(F32), 0.0)
    tail = jnp.where(row == base + 1, qb.astype(F32), tail)
    tail = jnp.where(row == base + 2, qc.astype(F32), tail)
    other = 3 - base
    tail = jnp.where((row >= other) & (row < other + 3), 1.0, tail)
    a, b, c = a.astype(F32), b.astype(F32), c.astype(F32)
    zero = jnp.zeros_like(tail)
    if left:
        return jnp.concatenate([a, a, b, b, a, c, tail, zero], axis=0)
    a, b, c = -2.0 * a, -2.0 * b, -2.0 * c
    return jnp.concatenate([a, b, a, b, c, a, tail, zero], axis=0)


def matern(s):
    s = jnp.maximum(s, 1e-30)
    dist = s * lax.rsqrt(s)
    shifted = dist + 1.5 / LN2
    return (shifted * shifted + 0.75 / LN2**2) * jnp.exp2(math.log2(LN2**2 / 3.0) - dist)


def make_kernel(rows_n, cols_n, own):
    span = rows_n * own
    wide = cols_n * own
    n_chunks = wide // CHUNK
    n_pieces = span // PIECE
    pair = CHUNK // own
    turns = n_chunks
    kept_n = n_pieces // turns

    def is_kept(piece, chunk):
        return (piece + chunk) % turns == 0

    def kept_at(piece, chunk):
        return chunk * kept_n + piece // turns

    def kernel(
        pts_ref, init_ref, targ_ref, scale_ref,
        sol_ref, res_ref, low_hbm,
        high, low, stage, left, right, vecs, acc_ref, first_own, first_all, right_all,
        vec_own, vec_all, part, part_all, dot_a, dot_a_all, dot_b, dot_b_all,
        col_send, col_recv, row_send, row_recv, stage_sem,
    ):
        my_row, my_col = lax.axis_index("row"), lax.axis_index("col")
        first_turn = lax.rem(my_row, turns)
        my_turn = lax.rem(my_col // pair - first_turn + turns, turns)
        my_slot = my_turn * (rows_n // turns) + my_row // turns
        my_place = my_turn * pair + lax.rem(my_col, pair)

        barrier = pltpu.get_barrier_semaphore()

        @pl.loop(1, rows_n)
        def _(k):
            pl.semaphore_signal(
                barrier, inc=1, device_id=(lax.rem(my_row + k, rows_n), my_col), device_id_type=MESH
            )

        @pl.loop(1, cols_n)
        def _(k):
            pl.semaphore_signal(
                barrier, inc=1, device_id=(my_row, lax.rem(my_col + k, cols_n)), device_id_type=MESH
            )

        z_own = pts_ref[...] / scale_ref[...] * DIST_SCALE
        first_own[0:VECS, :] = z_own
        first_own[VECS:, :] = init_ref[...]
        pl.semaphore_wait(barrier, rows_n - 1 + cols_n - 1)

        def to_rows(phase, src, dst, k, slot):
            return pltpu.make_async_remote_copy(
                src_ref=src, dst_ref=dst.at[slot],
                send_sem=row_send.at[phase, k], recv_sem=row_recv.at[phase, slot],
                device_id=(lax.rem(my_row + k, rows_n), my_col), device_id_type=MESH,
            )

        def to_cols(phase, src, dst, k, slot):
            return pltpu.make_async_remote_copy(
                src_ref=src, dst_ref=dst.at[slot],
                send_sem=col_send.at[phase, k], recv_sem=col_recv.at[phase, slot],
                device_id=(my_row, lax.rem(my_col + k, cols_n)), device_id_type=MESH,
            )

        def start_all(make, phase, src, dst, count, slot):
            @pl.loop(1, count)
            def _(k):
                make(phase, src, dst, k, slot).start()

        def sent_all(make, phase, src, dst, count):
            @pl.loop(1, count)
            def _(k):
                make(phase, src, dst, k, 0).wait_send()

        def arrived(make, phase, src, dst, slot, mine):
            @pl.when(slot != mine)
            def _():
                make(phase, src, dst, 1, slot).wait_recv()

        points_own = first_own.at[pl.ds(0, VECS)]
        start_all(to_cols, 0, points_own, right_all, cols_n, my_place)
        start_all(to_rows, 0, first_own, first_all, rows_n, my_slot)
        first_all[my_slot] = first_own[...]
        right_all[my_place] = z_own

        def put_vecs(slot, block):
            here = pl.ds(pl.multiple_of(slot * own, 128), own)
            a, b, c = split3(block)
            vecs[0:VECS, here] = a
            vecs[VECS:2 * VECS, here] = b
            vecs[2 * VECS:, here] = c

        def part_copy(call, owner, sender):
            k = lax.rem(owner - my_col + cols_n, cols_n)
            return to_cols(1 + call, part.at[call, owner], part_all.at[call], k, sender)

        def send_part(call, turn, acc):
            total = acc[0:VECS] + acc[VECS:2 * VECS] + acc[2 * VECS:3 * VECS] + acc[3 * VECS:]
            for n in range(pair):
                owner = lax.rem(first_turn + turn, turns) * pair + n
                part[call, owner] = total[:, n * own:(n + 1) * own]

                @pl.when(owner != my_col)
                def _():
                    part_copy(call, owner, my_col).start()

        def reduced(call, block):
            @pl.loop(1, cols_n)
            def _(k):
                part_copy(call, lax.rem(my_col + 1, cols_n), lax.rem(my_col + k, cols_n)).wait_recv()
            part_all[call, my_col] = part[call, my_col]
            total = part_all[call, 0]
            for slot in range(1, cols_n):
                total = total + part_all[call, slot]
            return total + NOISE_VAR * block

        def owner_step(call, turn):
            @pl.when(my_turn == turn)
            def _():
                if call == 0:
                    block = targ_ref[...] - reduced(0, init_ref[...])
                else:
                    block = reduced(1, vec_own[0])
                vec_own[call] = block
                vec_all[call, my_slot] = block
                start_all(to_rows, 1 + call, vec_own.at[call], vec_all.at[call], rows_n, my_slot)

        def take_piece(call, piece):
            for n in range(2):
                slot = piece * 2 + n
                arrived(to_rows, 1 + call, vec_own.at[call], vec_all.at[call], slot, my_slot)
                put_vecs(slot, vec_all[call, slot])

        @pl.loop(0, n_chunks)
        def _(chunk):
            cols = pl.ds(pl.multiple_of(chunk * CHUNK, CHUNK), CHUNK)
            for n in range(pair):
                place = chunk * pair + n
                arrived(to_cols, 0, points_own, right_all, place, my_place)
                right[:, pl.ds(pl.multiple_of(place * own, 128), own)] = stacked(right_all[place], False).astype(BF16)
            acc_ref[0] = jnp.zeros((4 * VECS, CHUNK), F32)

            @pl.loop(0, n_pieces)
            def _(turn):
                piece = lax.rem(my_slot // 2 + turn, n_pieces)

                @pl.when(chunk == 0)
                def _():
                    for n in range(2):
                        slot = piece * 2 + n
                        arrived(to_rows, 0, first_own, first_all, slot, my_slot)
                        here = pl.ds(pl.multiple_of(slot * own, 128), own)
                        left[here, :] = stacked(first_all[slot, 0:VECS], True).T.astype(BF16)
                        put_vecs(slot, first_all[slot, VECS:])

                count = chunk * n_pieces + turn
                slot = lax.rem(count, STAGES)

                @pl.when(count >= STAGES)
                def _():
                    pltpu.make_async_copy(stage.at[slot], low.at[0], stage_sem.at[slot]).wait()

                acc = acc_low = None
                for sub in range(PIECE // SUB):
                    rows = pl.ds(pl.multiple_of(piece * PIECE + sub * SUB, SUB), SUB)
                    m = matern(jnp.dot(left[rows, :], right[:, cols], preferred_element_type=F32))
                    h = m.astype(BF16)
                    l = (m - h.astype(F32)).astype(BF16)
                    high[rows, cols] = h
                    stage[slot, sub * SUB:(sub + 1) * SUB, :] = l
                    more = jnp.dot(vecs[:, rows], h, preferred_element_type=F32)
                    more_low = jnp.dot(vecs[0:VECS, rows], l, preferred_element_type=F32)
                    acc = more if acc is None else acc + more
                    acc_low = more_low if acc_low is None else acc_low + more_low
                acc_ref[0, 0:3 * VECS] += acc
                acc_ref[0, 3 * VECS:] += acc_low

                kept = is_kept(piece, chunk)

                @pl.when(kept)
                def _():
                    pltpu.make_async_copy(
                        stage.at[slot], low.at[kept_at(piece, chunk)], stage_sem.at[slot]
                    ).start()

                @pl.when(jnp.logical_not(kept))
                def _():
                    pltpu.make_async_copy(stage.at[slot], low_hbm.at[chunk, piece], stage_sem.at[slot]).start()

            send_part(0, chunk, acc_ref[0])
            for turn in range(n_chunks - 1):
                @pl.when(chunk == turn + 1)
                def _():
                    owner_step(0, turn)

        for slot in range(STAGES):
            pltpu.make_async_copy(stage.at[slot], low.at[0], stage_sem.at[slot]).wait()

        early = [(piece, chunk) for piece in range(EARLY) for chunk in range(n_chunks)]
        late = [(piece, chunk) for chunk in range(n_chunks) for piece in range(EARLY, n_pieces)]
        units = early + late
        far = [unit for unit in units if not is_kept(*unit)]

        def fetch(count):
            piece, chunk = far[count % len(far)]
            slot = count % STAGES
            return pltpu.make_async_copy(low_hbm.at[chunk, piece], stage.at[slot], stage_sem.at[slot])

        def product(call, fetched, last, hooks):
            for number, (piece, chunk) in enumerate(units):
                for hook in hooks.get(number, ()):
                    hook()
                if chunk == 0:
                    take_piece(call - 1, piece)
                rows = slice(piece * PIECE, (piece + 1) * PIECE)
                cols = slice(chunk * CHUNK, (chunk + 1) * CHUNK)
                acc = jnp.dot(vecs[:, rows], high[rows, cols], preferred_element_type=F32)
                if is_kept(piece, chunk):
                    below = low[kept_at(piece, chunk)]
                else:
                    fetch(fetched).wait()
                    below = stage[fetched % STAGES]
                acc_low = jnp.dot(vecs[0:VECS, rows], below, preferred_element_type=F32)
                if not is_kept(piece, chunk):
                    if not (last and fetched + STAGES >= 2 * len(far)):
                        fetch(fetched + STAGES).start()
                    fetched += 1
                if piece == 0:
                    acc_ref[chunk, 0:3 * VECS] = acc
                    acc_ref[chunk, 3 * VECS:] = acc_low
                else:
                    acc_ref[chunk, 0:3 * VECS] += acc
                    acc_ref[chunk, 3 * VECS:] += acc_low
                if piece == n_pieces - 1:
                    send_part(call, chunk, acc_ref[chunk])
            return fetched

        row_of = lax.broadcasted_iota(jnp.int32, (VECS, 128), 0)
        lane_of = lax.broadcasted_iota(jnp.int32, (VECS, 128), 1)

        def dots_local(phase, pairs):
            line = jnp.zeros((1, 128), F32)
            for n, (x, y) in enumerate(pairs):
                value = jnp.sum(x * y, axis=1, keepdims=True)
                here = lane_of == row_of + n * VECS
                line = line + jnp.sum(jnp.where(here, value, 0.0), axis=0, keepdims=True)
            block = jnp.broadcast_to(line, (8, 128))
            dot_a[phase] = block
            dot_a_all[phase, my_col] = block
            start_all(to_cols, 4 + phase, dot_a.at[phase], dot_a_all.at[phase], cols_n, my_col)

        def dots_row(phase):
            @pl.loop(1, cols_n)
            def _(k):
                slot = lax.rem(my_col + k, cols_n)
                to_cols(4 + phase, dot_a.at[phase], dot_a_all.at[phase], 1, slot).wait_recv()
            total = dot_a_all[phase, 0]
            for slot in range(1, cols_n):
                total = total + dot_a_all[phase, slot]
            dot_b[phase] = total
            dot_b_all[phase, my_row] = total
            start_all(to_rows, 3 + phase, dot_b.at[phase], dot_b_all.at[phase], rows_n, my_row)

        def dots_whole(phase, count):
            @pl.loop(1, rows_n)
            def _(k):
                slot = lax.rem(my_row + k, rows_n)
                to_rows(3 + phase, dot_b.at[phase], dot_b_all.at[phase], 1, slot).wait_recv()
            total = dot_b_all[phase, 0]
            for slot in range(1, rows_n):
                total = total + dot_b_all[phase, slot]
            line = jnp.broadcast_to(total[0:1], (VECS, 128))
            return [
                jnp.sum(jnp.where(lane_of == row_of + n * VECS, line, 0.0), axis=1, keepdims=True)
                for n in range(count)
            ]

        def sent_before():
            sent_all(to_cols, 0, points_own, right_all, cols_n)
            sent_all(to_rows, 0, first_own, first_all, rows_n)
            for call in range(2):
                sent_parts(call)
                sent_all(to_rows, 1 + call, vec_own.at[call], vec_all.at[call], rows_n)

        def sent_parts(call):
            @pl.loop(1, cols_n)
            def _(k):
                part_copy(call, lax.rem(my_col + k, cols_n), 0).wait_send()

        def hooks_after(call):
            found = {}
            for turn in range(n_chunks):
                done = len(early) + (turn + 1) * (n_pieces - EARLY)
                at = done + LAG - len(units)
                if call == 0:
                    at = LAG if turn == n_chunks - 1 else None
                if at is not None and at >= 0:
                    found.setdefault(at, []).append(lambda turn=turn: owner_step(call, turn))
            return found

        def hooks_within(call):
            found = {}
            for turn in range(n_chunks):
                done = len(early) + (turn + 1) * (n_pieces - EARLY)
                if done + LAG < len(units):
                    found.setdefault(done + LAG, []).append(lambda turn=turn: owner_step(call, turn))
            return found

        def merged(*tables):
            found = {}
            for table in tables:
                for at, hooks in table.items():
                    found.setdefault(at, []).extend(hooks)
            return found

        for count in range(STAGES):
            fetch(count).start()
        fetched = product(1, 0, False, merged(hooks_after(0), hooks_within(1)))
        fetched = product(2, fetched, True, merged(
            hooks_after(1),
            {
                14: [lambda: dots_local(0, [(vec_own[0], vec_own[0]), (vec_own[0], vec_own[1])])],
                18: [sent_before],
                26: [lambda: dots_row(0)],
            },
        ))
        res0, image0 = vec_own[0], vec_own[1]
        norm0, curve0 = dots_whole(0, 2)
        alpha0 = norm0 / curve0
        res1 = res0 - alpha0 * image0
        image1 = reduced(2, image0)
        half = image0 - alpha0 * image1
        dots_local(1, [(res1, res1), (res1, half), (res1 + res1, image0)])
        dots_row(1)
        norm1, own_curve, cross = dots_whole(1, 3)
        beta0 = norm1 / norm0
        curve1 = own_curve + beta0 * cross + beta0 * beta0 * curve0
        alpha1 = norm1 / curve1
        sol_ref[...] = init_ref[...] + alpha0 * res0 + alpha1 * (res1 + beta0 * res0)
        res_ref[...] = res1 - alpha1 * (half + beta0 * image0)
        sent_parts(2)
        for phase in range(2):
            sent_all(to_cols, 4 + phase, dot_a.at[phase], dot_a_all.at[phase], cols_n)
            sent_all(to_rows, 3 + phase, dot_b.at[phase], dot_b_all.at[phase], rows_n)

    def scratch():
        return [
            pltpu.VMEM((span, wide), BF16),
            pltpu.VMEM((n_chunks * kept_n, PIECE, CHUNK), BF16),
            pltpu.VMEM((STAGES, PIECE, CHUNK), BF16),
            pltpu.VMEM((span, DEPTH), BF16),
            pltpu.VMEM((DEPTH, wide), BF16),
            pltpu.VMEM((3 * VECS, span), BF16),
            pltpu.VMEM((n_chunks, 4 * VECS, CHUNK), F32),
            pltpu.VMEM((2 * VECS, own), F32),
            pltpu.VMEM((rows_n, 2 * VECS, own), F32),
            pltpu.VMEM((cols_n, VECS, own), F32),
            pltpu.VMEM((2, VECS, own), F32),
            pltpu.VMEM((2, rows_n, VECS, own), F32),
            pltpu.VMEM((3, cols_n, VECS, own), F32),
            pltpu.VMEM((3, cols_n, VECS, own), F32),
            pltpu.VMEM((2, 8, 128), F32),
            pltpu.VMEM((2, cols_n, 8, 128), F32),
            pltpu.VMEM((2, 8, 128), F32),
            pltpu.VMEM((2, rows_n, 8, 128), F32),
            pltpu.SemaphoreType.DMA((6, cols_n)),
            pltpu.SemaphoreType.DMA((6, cols_n)),
            pltpu.SemaphoreType.DMA((5, rows_n)),
            pltpu.SemaphoreType.DMA((5, rows_n)),
            pltpu.SemaphoreType.DMA((STAGES,)),
        ]

    vmem = pl.BlockSpec(memory_space=pltpu.VMEM)
    return pl.pallas_call(
        kernel,
        out_shape=[
            jax.ShapeDtypeStruct((VECS, own), F32),
            jax.ShapeDtypeStruct((VECS, own), F32),
            jax.ShapeDtypeStruct((n_chunks, n_pieces, PIECE, CHUNK), BF16),
        ],
        in_specs=[vmem] * 4,
        out_specs=[vmem, vmem, pl.BlockSpec(memory_space=pl.ANY)],
        scratch_shapes=scratch(),
        compiler_params=pltpu.CompilerParams(
            collective_id=0, has_side_effects=True, vmem_limit_bytes=60 * 2**20
        ),
        name="conjugate_gradients",
    )


def solution(mesh):
    rows_n, cols_n = mesh.shape["row"], mesh.shape["col"]

    def shards(points, targets, initial, lengthscale):
        call = make_kernel(rows_n, cols_n, points.shape[0])
        sol, res, _ = call(points.T, initial.T, targets.T, lengthscale[:, None])
        return sol.T, res.T

    spec = P(("row", "col"), None)
    return jax.shard_map(
        shards, mesh=mesh, in_specs=(spec, spec, spec, P()), out_specs=(spec, spec), check_vma=False
    )
```

```python
import math

import jax
import jax.numpy as jnp
from jax import lax
from jax.experimental import pallas as pl
from jax.experimental.pallas import tpu as pltpu
from jax.sharding import PartitionSpec as P

MESH = pl.DeviceIdType.MESH
F32, BF16 = jnp.float32, jnp.bfloat16
NOISE_VAR = 0.5
LN2 = math.log(2.0)
DIST_SCALE = math.sqrt(5.0) / LN2
VECS = 16
DEPTH = 128
CHUNK = 768
PIECE = 768
GROUP = 2 * PIECE
SUB = 512
STAGES = 4
EARLY = 3
LAG = 7


def split3(x):
    first = x.astype(BF16)
    rest = x - first.astype(F32)
    second = rest.astype(BF16)
    third = (rest - second.astype(F32)).astype(BF16)
    return first, second, third


def stacked(z, left):
    a, b, c = split3(z)
    qa, qb, qc = split3(jnp.sum(z * z, axis=0, keepdims=True))
    row = lax.broadcasted_iota(jnp.int32, z.shape, 0)
    base = 0 if left else 3
    tail = jnp.where(row == base, qa.astype(F32), 0.0)
    tail = jnp.where(row == base + 1, qb.astype(F32), tail)
    tail = jnp.where(row == base + 2, qc.astype(F32), tail)
    other = 3 - base
    tail = jnp.where((row >= other) & (row < other + 3), 1.0, tail)
    a, b, c = a.astype(F32), b.astype(F32), c.astype(F32)
    zero = jnp.zeros_like(tail)
    if left:
        return jnp.concatenate([a, a, b, b, a, c, tail, zero], axis=0)
    a, b, c = -2.0 * a, -2.0 * b, -2.0 * c
    return jnp.concatenate([a, b, a, b, c, a, tail, zero], axis=0)


def matern(s):
    s = jnp.maximum(s, 1e-30)
    dist = s * lax.rsqrt(s)
    shifted = dist + 1.5 / LN2
    return (shifted * shifted + 0.75 / LN2**2) * jnp.exp2(math.log2(LN2**2 / 3.0) - dist)


def make_kernel(rows_n, cols_n, own):
    span = rows_n * own
    wide = cols_n * own
    n_chunks = wide // CHUNK
    n_pieces = span // PIECE
    pair = CHUNK // own
    turns = n_chunks
    each = rows_n // turns

    def is_kept(group, chunk):
        return (group + chunk) % turns == 0

    def kernel(
        pts_ref, init_ref, targ_ref, scale_ref,
        out_ref, low_hbm,
        high, low, stage, left, right, vecs, acc_ref, first_own, first_all, right_all,
        vec_own, vec_all, col_all, part, part_all, dot_a, dot_a_all, dot_b, dot_b_all,
        col_send, col_recv, row_send, row_recv, stage_sem,
    ):
        my_row, my_col = lax.axis_index("row"), lax.axis_index("col")
        first_turn = lax.rem(my_row, turns)
        my_turn = lax.rem(my_col // pair - first_turn + turns, turns)
        my_slot = my_turn * each + my_row // turns
        my_place = my_turn * pair + lax.rem(my_col, pair)

        barrier = pltpu.get_barrier_semaphore()

        @pl.loop(1, rows_n)
        def _(k):
            pl.semaphore_signal(
                barrier, inc=1, device_id=(lax.rem(my_row + k, rows_n), my_col), device_id_type=MESH
            )

        @pl.loop(1, cols_n)
        def _(k):
            pl.semaphore_signal(
                barrier, inc=1, device_id=(my_row, lax.rem(my_col + k, cols_n)), device_id_type=MESH
            )

        square = (VECS, VECS)
        on_diagonal = lax.broadcasted_iota(jnp.int32, square, 0) == lax.broadcasted_iota(jnp.int32, square, 1)
        scales = jnp.broadcast_to(scale_ref[...], square)
        scale = jnp.sum(jnp.where(on_diagonal, scales, 0.0), axis=1, keepdims=True)
        z_own = pts_ref[...] / scale * DIST_SCALE
        first_own[0:VECS, :] = z_own
        first_own[VECS:, :] = init_ref[...]
        pl.semaphore_wait(barrier, rows_n - 1 + cols_n - 1)

        def to_rows(phase, src, dst, k, slot):
            return pltpu.make_async_remote_copy(
                src_ref=src, dst_ref=dst.at[slot],
                send_sem=row_send.at[phase, k], recv_sem=row_recv.at[phase, slot],
                device_id=(lax.rem(my_row + k, rows_n), my_col), device_id_type=MESH,
            )

        def to_cols(phase, src, dst, k, slot):
            return pltpu.make_async_remote_copy(
                src_ref=src, dst_ref=dst.at[slot],
                send_sem=col_send.at[phase, k], recv_sem=col_recv.at[phase, slot],
                device_id=(my_row, lax.rem(my_col + k, cols_n)), device_id_type=MESH,
            )

        def start_all(make, phase, src, dst, count, slot):
            @pl.loop(1, count)
            def _(k):
                make(phase, src, dst, k, slot).start()

        def sent_all(make, phase, src, dst, count):
            @pl.loop(1, count)
            def _(k):
                make(phase, src, dst, k, 0).wait_send()

        def arrived(make, phase, src, dst, slot, mine):
            @pl.when(slot != mine)
            def _():
                make(phase, src, dst, 1, slot).wait_recv()

        points_own = first_own.at[pl.ds(0, VECS)]
        for n in range(1, each):
            to_rows(0, first_own, first_all, n * turns, my_slot).start()

        @pl.when(my_turn == 0)
        def _():
            start_all(to_cols, 0, points_own, right_all, cols_n, my_place)

        def send_group(turn):
            @pl.loop(0, each)
            def _(n):
                to_rows(0, first_own, first_all, n * turns + turn, my_slot).start()

        send_group(1)
        first_all[my_slot] = first_own[...]
        right_all[my_place] = z_own

        def put_vecs(slot, block):
            here = pl.ds(pl.multiple_of(slot * own, 128), own)
            a, b, c = split3(block)
            vecs[0:VECS, here] = a
            vecs[VECS:2 * VECS, here] = b
            vecs[2 * VECS:, here] = c

        def part_copy(call, owner, sender):
            k = lax.rem(owner - my_col + cols_n, cols_n)
            return to_cols(1 + call, part.at[call, owner], part_all.at[call], k, sender)

        def send_part(call, turn, acc):
            total = acc[0:VECS] + acc[VECS:2 * VECS] + acc[2 * VECS:3 * VECS] + acc[3 * VECS:]
            for n in range(pair):
                owner = lax.rem(first_turn + turn, turns) * pair + n
                part[call, owner] = total[:, n * own:(n + 1) * own]

                @pl.when(owner != my_col)
                def _():
                    part_copy(call, owner, my_col).start()

        def reduced(call, block):
            @pl.loop(1, cols_n)
            def _(k):
                part_copy(call, lax.rem(my_col + 1, cols_n), lax.rem(my_col + k, cols_n)).wait_recv()
            part_all[call, my_col] = part[call, my_col]
            total = part_all[call, 0]
            for slot in range(1, cols_n):
                total = total + part_all[call, slot]
            return total + NOISE_VAR * block

        def owner_step(call, turn):
            @pl.when(my_turn == turn)
            def _():
                if call == 0:
                    block = targ_ref[...] - reduced(0, init_ref[...])
                else:
                    block = reduced(1, vec_own[0])
                vec_own[call] = block
                vec_all[call, my_slot] = block
                start_all(to_rows, 1 + call, vec_own.at[call], vec_all.at[call], rows_n, my_slot)
                col_all[call, my_place] = block
                start_all(to_cols, 6 + call, vec_own.at[call], col_all.at[call], cols_n, my_place)

        def take_piece(call, piece):
            for n in range(2):
                slot = piece * 2 + n
                arrived(to_rows, 1 + call, vec_own.at[call], vec_all.at[call], slot, my_slot)
                put_vecs(slot, vec_all[call, slot])

        @pl.loop(0, n_chunks)
        def _(chunk):
            cols = pl.ds(pl.multiple_of(chunk * CHUNK, CHUNK), CHUNK)
            for n in range(pair):
                place = chunk * pair + n
                arrived(to_cols, 0, points_own, right_all, place, my_place)
                right[:, pl.ds(pl.multiple_of(place * own, 128), own)] = stacked(right_all[place], False).astype(BF16)
            acc_ref[0] = jnp.zeros((4 * VECS, CHUNK), F32)

            @pl.loop(0, turns)
            def _(turn):
                group = lax.rem(my_turn + turn, turns)

                @pl.when(chunk == 0)
                def _():
                    for n in range(each):
                        slot = group * each + n
                        arrived(to_rows, 0, first_own, first_all, slot, my_slot)
                        here = pl.ds(pl.multiple_of(slot * own, 128), own)
                        left[here, :] = stacked(first_all[slot, 0:VECS], True).T.astype(BF16)
                        put_vecs(slot, first_all[slot, VECS:])

                    @pl.when(turn + 2 < turns)
                    def _():
                        send_group(turn + 2)

                    @pl.when((turn == 0) & (my_turn != 0))
                    def _():
                        start_all(to_cols, 0, points_own, right_all, cols_n, my_place)

                count = chunk * turns + turn
                half = pl.ds(pl.multiple_of(lax.rem(count, 2) * GROUP, GROUP), GROUP)
                sem = stage_sem.at[lax.rem(count, 2)]

                @pl.when(count >= 2)
                def _():
                    pltpu.make_async_copy(stage.at[half], low.at[0], sem).wait()

                acc = acc_low = None
                for sub in range(GROUP // SUB):
                    rows = pl.ds(pl.multiple_of(group * GROUP + sub * SUB, SUB), SUB)
                    m = matern(jnp.dot(left[rows, :], right[:, cols], preferred_element_type=F32))
                    h = m.astype(BF16)
                    l = (m - h.astype(F32)).astype(BF16)
                    high[rows, cols] = h
                    stage[pl.ds(pl.multiple_of(lax.rem(count, 2) * GROUP + sub * SUB, SUB), SUB), :] = l
                    more = jnp.dot(vecs[:, rows], h, preferred_element_type=F32)
                    more_low = jnp.dot(vecs[0:VECS, rows], l, preferred_element_type=F32)
                    acc = more if acc is None else acc + more
                    acc_low = more_low if acc_low is None else acc_low + more_low
                acc_ref[0, 0:3 * VECS] += acc
                acc_ref[0, 3 * VECS:] += acc_low

                kept = is_kept(group, chunk)

                @pl.when(kept)
                def _():
                    pltpu.make_async_copy(stage.at[half], low.at[chunk], sem).start()

                @pl.when(jnp.logical_not(kept))
                def _():
                    pltpu.make_async_copy(stage.at[half], low_hbm.at[chunk, group], sem).start()

            send_part(0, chunk, acc_ref[0])
            for turn in range(n_chunks - 1):
                @pl.when(chunk == turn + 1)
                def _():
                    owner_step(0, turn)

        for n in range(2):
            pltpu.make_async_copy(stage.at[pl.ds(n * GROUP, GROUP)], low.at[0], stage_sem.at[n]).wait()

        early = [(piece, chunk) for piece in range(EARLY) for chunk in range(n_chunks)]
        late = [(piece, chunk) for chunk in range(n_chunks) for piece in range(EARLY, n_pieces)]
        units = early + late
        far = [(piece, chunk) for piece, chunk in units if not is_kept(piece // 2, chunk)]

        def fetch(count):
            piece, chunk = far[count % len(far)]
            slot = count % STAGES
            away = low_hbm.at[chunk, piece // 2, pl.ds(piece % 2 * PIECE, PIECE)]
            return pltpu.make_async_copy(away, stage.at[pl.ds(slot * PIECE, PIECE)], stage_sem.at[slot])

        def product(call, fetched, last, hooks):
            for number, (piece, chunk) in enumerate(units):
                for hook in hooks.get(number, ()):
                    hook()
                if chunk == 0:
                    take_piece(call - 1, piece)
                rows = slice(piece * PIECE, (piece + 1) * PIECE)
                cols = slice(chunk * CHUNK, (chunk + 1) * CHUNK)
                acc = jnp.dot(vecs[:, rows], high[rows, cols], preferred_element_type=F32)
                if is_kept(piece // 2, chunk):
                    below = low[chunk, piece % 2 * PIECE:(piece % 2 + 1) * PIECE]
                else:
                    fetch(fetched).wait()
                    below = stage[fetched % STAGES * PIECE:(fetched % STAGES + 1) * PIECE]
                acc_low = jnp.dot(vecs[0:VECS, rows], below, preferred_element_type=F32)
                if not is_kept(piece // 2, chunk):
                    if not (last and fetched + STAGES >= 2 * len(far)):
                        fetch(fetched + STAGES).start()
                    fetched += 1
                if piece == 0:
                    acc_ref[chunk, 0:3 * VECS] = acc
                    acc_ref[chunk, 3 * VECS:] = acc_low
                else:
                    acc_ref[chunk, 0:3 * VECS] += acc
                    acc_ref[chunk, 3 * VECS:] += acc_low
                if piece == n_pieces - 1:
                    send_part(call, chunk, acc_ref[chunk])
            return fetched

        row_of = lax.broadcasted_iota(jnp.int32, (VECS, 128), 0)
        lane_of = lax.broadcasted_iota(jnp.int32, (VECS, 128), 1)

        def dots_local(phase, values):
            line = jnp.zeros((1, 128), F32)
            for n, value in enumerate(values):
                here = lane_of == row_of + n * VECS
                line = line + jnp.sum(jnp.where(here, value, 0.0), axis=0, keepdims=True)
            block = jnp.broadcast_to(line, (8, 128))
            dot_a[phase] = block
            dot_a_all[phase, my_col] = block
            start_all(to_cols, 4 + phase, dot_a.at[phase], dot_a_all.at[phase], cols_n, my_col)

        def dot(x, y):
            return jnp.sum(x * y, axis=1, keepdims=True)

        def dots_row(phase):
            @pl.loop(1, cols_n)
            def _(k):
                slot = lax.rem(my_col + k, cols_n)
                to_cols(4 + phase, dot_a.at[phase], dot_a_all.at[phase], 1, slot).wait_recv()
            total = dot_a_all[phase, 0]
            for slot in range(1, cols_n):
                total = total + dot_a_all[phase, slot]
            dot_b[phase] = total
            dot_b_all[phase, my_row] = total
            start_all(to_rows, 3 + phase, dot_b.at[phase], dot_b_all.at[phase], rows_n, my_row)

        def dots_whole(phase, count):
            @pl.loop(1, rows_n)
            def _(k):
                slot = lax.rem(my_row + k, rows_n)
                to_rows(3 + phase, dot_b.at[phase], dot_b_all.at[phase], 1, slot).wait_recv()
            total = dot_b_all[phase, 0]
            for slot in range(1, rows_n):
                total = total + dot_b_all[phase, slot]
            line = jnp.broadcast_to(total[0:1], (VECS, 128))
            return [
                jnp.sum(jnp.where(lane_of == row_of + n * VECS, line, 0.0), axis=1, keepdims=True)
                for n in range(count)
            ]

        def sent_before():
            sent_all(to_cols, 0, points_own, right_all, cols_n)
            sent_all(to_rows, 0, first_own, first_all, rows_n)
            for call in range(2):
                sent_parts(call)
                sent_all(to_rows, 1 + call, vec_own.at[call], vec_all.at[call], rows_n)
                sent_all(to_cols, 6 + call, vec_own.at[call], col_all.at[call], cols_n)
                for place in range(cols_n):
                    arrived(to_cols, 6 + call, vec_own.at[call], col_all.at[call], place, my_place)

        def sent_parts(call):
            @pl.loop(1, cols_n)
            def _(k):
                part_copy(call, lax.rem(my_col + k, cols_n), 0).wait_send()

        def hooks_after(call):
            found = {}
            for turn in range(n_chunks):
                done = len(early) + (turn + 1) * (n_pieces - EARLY)
                at = done + LAG - len(units)
                if call == 0:
                    at = LAG if turn == n_chunks - 1 else None
                if at is not None and at >= 0:
                    found.setdefault(at, []).append(lambda turn=turn: owner_step(call, turn))
            return found

        def hooks_within(call):
            found = {}
            for turn in range(n_chunks):
                done = len(early) + (turn + 1) * (n_pieces - EARLY)
                if done + LAG < len(units):
                    found.setdefault(done + LAG, []).append(lambda turn=turn: owner_step(call, turn))
            return found

        def merged(*tables):
            found = {}
            for table in tables:
                for at, hooks in table.items():
                    found.setdefault(at, []).extend(hooks)
            return found

        for count in range(STAGES):
            fetch(count).start()
        fetched = product(1, 0, False, merged(hooks_after(0), hooks_within(1)))
        fetched = product(2, fetched, True, merged(
            hooks_after(1),
            {
                14: [lambda: dots_local(0, [dot(vec_own[0], vec_own[0]), dot(vec_own[0], vec_own[1])])],
                18: [sent_before],
                26: [lambda: dots_row(0)],
            },
        ))
        res0, image0 = vec_own[0], vec_own[1]
        norm0, curve0 = dots_whole(0, 2)
        alpha0 = norm0 / curve0
        res1 = res0 - alpha0 * image0
        crossed = jnp.zeros((VECS, own), F32)
        for place in range(cols_n):
            owner = lax.rem(first_turn + place // pair, turns) * pair + place % pair
            there = col_all[0, place] - alpha0 * col_all[1, place]
            crossed = crossed + there * part[2, owner]
        dots_local(1, [dot(res1, res1), dot(res1, image0), jnp.sum(crossed, axis=1, keepdims=True)])
        dots_row(1)
        image1 = reduced(2, image0)
        half = image0 - alpha0 * image1
        norm1, cross, crossed = dots_whole(1, 3)
        own_curve = cross - alpha0 * (crossed + NOISE_VAR * cross)
        beta0 = norm1 / norm0
        curve1 = own_curve + 2.0 * beta0 * cross + beta0 * beta0 * curve0
        alpha1 = norm1 / curve1
        out_ref[0] = init_ref[...] + alpha0 * res0
        out_ref[1] = alpha1 * (res1 + beta0 * res0)
        out_ref[2] = res1
        out_ref[3] = -alpha1 * (half + beta0 * image0)
        sent_parts(2)
        for phase in range(2):
            sent_all(to_cols, 4 + phase, dot_a.at[phase], dot_a_all.at[phase], cols_n)
            sent_all(to_rows, 3 + phase, dot_b.at[phase], dot_b_all.at[phase], rows_n)

    def scratch():
        return [
            pltpu.VMEM((span, wide), BF16),
            pltpu.VMEM((n_chunks, GROUP, CHUNK), BF16),
            pltpu.VMEM((STAGES * PIECE, CHUNK), BF16),
            pltpu.VMEM((span, DEPTH), BF16),
            pltpu.VMEM((DEPTH, wide), BF16),
            pltpu.VMEM((3 * VECS, span), BF16),
            pltpu.VMEM((n_chunks, 4 * VECS, CHUNK), F32),
            pltpu.VMEM((2 * VECS, own), F32),
            pltpu.VMEM((rows_n, 2 * VECS, own), F32),
            pltpu.VMEM((cols_n, VECS, own), F32),
            pltpu.VMEM((2, VECS, own), F32),
            pltpu.VMEM((2, rows_n, VECS, own), F32),
            pltpu.VMEM((2, cols_n, VECS, own), F32),
            pltpu.VMEM((3, cols_n, VECS, own), F32),
            pltpu.VMEM((3, cols_n, VECS, own), F32),
            pltpu.VMEM((2, 8, 128), F32),
            pltpu.VMEM((2, cols_n, 8, 128), F32),
            pltpu.VMEM((2, 8, 128), F32),
            pltpu.VMEM((2, rows_n, 8, 128), F32),
            pltpu.SemaphoreType.DMA((8, cols_n)),
            pltpu.SemaphoreType.DMA((8, cols_n)),
            pltpu.SemaphoreType.DMA((5, rows_n)),
            pltpu.SemaphoreType.DMA((5, rows_n)),
            pltpu.SemaphoreType.DMA((STAGES,)),
        ]

    vmem = pl.BlockSpec(memory_space=pltpu.VMEM)
    return pl.pallas_call(
        kernel,
        out_shape=[
            jax.ShapeDtypeStruct((4, VECS, own), F32),
            jax.ShapeDtypeStruct((n_chunks, turns, GROUP, CHUNK), BF16),
        ],
        in_specs=[vmem] * 4,
        out_specs=[vmem, pl.BlockSpec(memory_space=pl.ANY)],
        scratch_shapes=scratch(),
        compiler_params=pltpu.CompilerParams(
            collective_id=0, has_side_effects=True, vmem_limit_bytes=63 * 2**20
        ),
        name="conjugate_gradients",
    )


def solution(mesh):
    rows_n, cols_n = mesh.shape["row"], mesh.shape["col"]

    def shards(points, targets, initial, lengthscale):
        call = make_kernel(rows_n, cols_n, points.shape[0])
        out, _ = call(points.T, initial.T, targets.T, lengthscale[None, :])
        return (out[0] + out[1]).T, (out[2] + out[3]).T

    spec = P(("row", "col"), None)
    return jax.shard_map(
        shards, mesh=mesh, in_specs=(spec, spec, spec, P()), out_specs=(spec, spec), check_vma=False
    )
```

```python
import math

import jax
import jax.numpy as jnp
from jax import lax
from jax.experimental import pallas as pl
from jax.experimental.pallas import tpu as pltpu
from jax.sharding import PartitionSpec as P

MESH = pl.DeviceIdType.MESH
F32, BF16 = jnp.float32, jnp.bfloat16
NOISE_VAR = 0.5
LN2 = math.log(2.0)
DIST_SCALE = math.sqrt(5.0) / LN2
VECS = 16
DEPTH = 128
CHUNK = 768
PIECE = 768
GROUP = 2 * PIECE
SUB = 768
TILE = 256
STAGES = 4
EARLY = 3
LAG = 7


def split3(x):
    first = x.astype(BF16)
    rest = x - first.astype(F32)
    second = rest.astype(BF16)
    third = (rest - second.astype(F32)).astype(BF16)
    return first, second, third


def stacked(z, left):
    a, b, c = split3(z)
    qa, qb, qc = split3(jnp.sum(z * z, axis=0, keepdims=True))
    row = lax.broadcasted_iota(jnp.int32, z.shape, 0)
    base = 0 if left else 3
    tail = jnp.where(row == base, qa.astype(F32), 0.0)
    tail = jnp.where(row == base + 1, qb.astype(F32), tail)
    tail = jnp.where(row == base + 2, qc.astype(F32), tail)
    other = 3 - base
    tail = jnp.where((row >= other) & (row < other + 3), 1.0, tail)
    a, b, c = a.astype(F32), b.astype(F32), c.astype(F32)
    zero = jnp.zeros_like(tail)
    if left:
        return jnp.concatenate([a, a, b, b, a, c, tail, zero], axis=0)
    a, b, c = -2.0 * a, -2.0 * b, -2.0 * c
    return jnp.concatenate([a, b, a, b, c, a, tail, zero], axis=0)


def matern(s):
    s = jnp.maximum(s, 1e-30)
    dist = s * lax.rsqrt(s)
    shifted = dist + 1.5 / LN2
    return (shifted * shifted + 0.75 / LN2**2) * jnp.exp2(math.log2(LN2**2 / 3.0) - dist)


def make_kernel(rows_n, cols_n, own):
    span = rows_n * own
    wide = cols_n * own
    n_chunks = wide // CHUNK
    n_pieces = span // PIECE
    pair = CHUNK // own
    turns = n_chunks
    each = rows_n // turns

    def is_kept(group, chunk):
        return (group + chunk) % turns == 0

    def kernel(
        pts_ref, init_ref, targ_ref, scale_ref,
        out_ref, low_hbm,
        high, low, stage, left, right, vecs, acc_ref, first_own, first_all, right_all,
        vec_own, vec_all, col_all, part, part_all, dot_a, dot_a_all, dot_b, dot_b_all,
        col_send, col_recv, row_send, row_recv, stage_sem,
    ):
        my_row, my_col = lax.axis_index("row"), lax.axis_index("col")
        first_turn = lax.rem(my_row, turns)
        my_turn = lax.rem(my_col // pair - first_turn + turns, turns)
        my_slot = my_turn * each + my_row // turns
        my_place = my_turn * pair + lax.rem(my_col, pair)

        barrier = pltpu.get_barrier_semaphore()

        @pl.loop(1, rows_n)
        def _(k):
            pl.semaphore_signal(
                barrier, inc=1, device_id=(lax.rem(my_row + k, rows_n), my_col), device_id_type=MESH
            )

        @pl.loop(1, cols_n)
        def _(k):
            pl.semaphore_signal(
                barrier, inc=1, device_id=(my_row, lax.rem(my_col + k, cols_n)), device_id_type=MESH
            )

        square = (VECS, VECS)
        on_diagonal = lax.broadcasted_iota(jnp.int32, square, 0) == lax.broadcasted_iota(jnp.int32, square, 1)
        scales = jnp.broadcast_to(scale_ref[...], square)
        scale = jnp.sum(jnp.where(on_diagonal, scales, 0.0), axis=1, keepdims=True)
        z_own = pts_ref[...] / scale * DIST_SCALE
        first_own[0:VECS, :] = z_own
        first_own[VECS:, :] = init_ref[...]
        pl.semaphore_wait(barrier, rows_n - 1 + cols_n - 1)

        def to_rows(phase, src, dst, k, slot):
            return pltpu.make_async_remote_copy(
                src_ref=src, dst_ref=dst.at[slot],
                send_sem=row_send.at[phase, k], recv_sem=row_recv.at[phase, slot],
                device_id=(lax.rem(my_row + k, rows_n), my_col), device_id_type=MESH,
            )

        def to_cols(phase, src, dst, k, slot):
            return pltpu.make_async_remote_copy(
                src_ref=src, dst_ref=dst.at[slot],
                send_sem=col_send.at[phase, k], recv_sem=col_recv.at[phase, slot],
                device_id=(my_row, lax.rem(my_col + k, cols_n)), device_id_type=MESH,
            )

        def start_all(make, phase, src, dst, count, slot):
            @pl.loop(1, count)
            def _(k):
                make(phase, src, dst, k, slot).start()

        def sent_all(make, phase, src, dst, count):
            @pl.loop(1, count)
            def _(k):
                make(phase, src, dst, k, 0).wait_send()

        def arrived(make, phase, src, dst, slot, mine):
            @pl.when(slot != mine)
            def _():
                make(phase, src, dst, 1, slot).wait_recv()

        points_own = first_own.at[pl.ds(0, VECS)]
        for n in range(1, each):
            to_rows(0, first_own, first_all, n * turns, my_slot).start()

        @pl.when(my_turn == 0)
        def _():
            start_all(to_cols, 0, points_own, right_all, cols_n, my_place)

        def send_group(turn):
            @pl.loop(0, each)
            def _(n):
                to_rows(0, first_own, first_all, n * turns + turn, my_slot).start()

        send_group(1)
        first_all[my_slot] = first_own[...]
        right_all[my_place] = z_own

        def put_vecs(slot, block):
            here = pl.ds(pl.multiple_of(slot * own, 128), own)
            a, b, c = split3(block)
            vecs[0:VECS, here] = a
            vecs[VECS:2 * VECS, here] = b
            vecs[2 * VECS:, here] = c

        def part_copy(call, owner, sender):
            k = lax.rem(owner - my_col + cols_n, cols_n)
            return to_cols(1 + call, part.at[call, owner], part_all.at[call], k, sender)

        def send_part(call, turn, acc):
            total = acc[0:VECS] + acc[VECS:2 * VECS] + acc[2 * VECS:3 * VECS] + acc[3 * VECS:]
            for n in range(pair):
                owner = lax.rem(first_turn + turn, turns) * pair + n
                part[call, owner] = total[:, n * own:(n + 1) * own]

                @pl.when(owner != my_col)
                def _():
                    part_copy(call, owner, my_col).start()

        def reduced(call, block):
            @pl.loop(1, cols_n)
            def _(k):
                part_copy(call, lax.rem(my_col + 1, cols_n), lax.rem(my_col + k, cols_n)).wait_recv()
            part_all[call, my_col] = part[call, my_col]
            total = part_all[call, 0]
            for slot in range(1, cols_n):
                total = total + part_all[call, slot]
            return total + NOISE_VAR * block

        def owner_step(call, turn):
            @pl.when(my_turn == turn)
            def _():
                if call == 0:
                    block = targ_ref[...] - reduced(0, init_ref[...])
                else:
                    block = reduced(1, vec_own[0])
                vec_own[call] = block
                vec_all[call, my_slot] = block
                start_all(to_rows, 1 + call, vec_own.at[call], vec_all.at[call], rows_n, my_slot)
                col_all[call, my_place] = block

        def spread_cols(call):
            start_all(to_cols, 6 + call, vec_own.at[call], col_all.at[call], cols_n, my_place)

        def take_piece(call, piece):
            for n in range(2):
                slot = piece * 2 + n
                arrived(to_rows, 1 + call, vec_own.at[call], vec_all.at[call], slot, my_slot)
                put_vecs(slot, vec_all[call, slot])

        @pl.loop(0, n_chunks)
        def _(chunk):
            for n in range(pair):
                place = chunk * pair + n
                arrived(to_cols, 0, points_own, right_all, place, my_place)
                right[:, pl.ds(pl.multiple_of(place * own, 128), own)] = stacked(right_all[place], False).astype(BF16)
            acc_ref[0] = jnp.zeros((4 * VECS, CHUNK), F32)

            @pl.loop(0, turns)
            def _(turn):
                group = lax.rem(my_turn + turn, turns)

                @pl.when(chunk == 0)
                def _():
                    for n in range(each):
                        slot = group * each + n
                        arrived(to_rows, 0, first_own, first_all, slot, my_slot)
                        here = pl.ds(pl.multiple_of(slot * own, 128), own)
                        left[here, :] = stacked(first_all[slot, 0:VECS], True).T.astype(BF16)
                        put_vecs(slot, first_all[slot, VECS:])

                    @pl.when(turn + 2 < turns)
                    def _():
                        send_group(turn + 2)

                    @pl.when((turn == 0) & (my_turn != 0))
                    def _():
                        start_all(to_cols, 0, points_own, right_all, cols_n, my_place)

                count = chunk * turns + turn
                half = pl.ds(pl.multiple_of(lax.rem(count, 2) * GROUP, GROUP), GROUP)
                sem = stage_sem.at[lax.rem(count, 2)]

                @pl.when(count >= 2)
                def _():
                    pltpu.make_async_copy(stage.at[half], low.at[0], sem).wait()

                for sub in range(GROUP // SUB):
                    rows = pl.ds(pl.multiple_of(group * GROUP + sub * SUB, SUB), SUB)
                    staged = pl.ds(pl.multiple_of(lax.rem(count, 2) * GROUP + sub * SUB, SUB), SUB)
                    for n in range(0, CHUNK, TILE):
                        here = pl.ds(pl.multiple_of(chunk * CHUNK + n, TILE), TILE)
                        m = matern(jnp.dot(left[rows, :], right[:, here], preferred_element_type=F32))
                        h = m.astype(BF16)
                        l = (m - h.astype(F32)).astype(BF16)
                        high[rows, here] = h
                        stage[staged, n:n + TILE] = l
                        acc_ref[0, 0:3 * VECS, n:n + TILE] += jnp.dot(vecs[:, rows], h, preferred_element_type=F32)
                        acc_ref[0, 3 * VECS:, n:n + TILE] += jnp.dot(vecs[0:VECS, rows], l, preferred_element_type=F32)

                kept = is_kept(group, chunk)

                @pl.when(kept)
                def _():
                    pltpu.make_async_copy(stage.at[half], low.at[chunk], sem).start()

                @pl.when(jnp.logical_not(kept))
                def _():
                    pltpu.make_async_copy(stage.at[half], low_hbm.at[chunk, group], sem).start()

            send_part(0, chunk, acc_ref[0])
            for turn in range(n_chunks - 1):
                @pl.when(chunk == turn + 1)
                def _():
                    owner_step(0, turn)

        for n in range(2):
            pltpu.make_async_copy(stage.at[pl.ds(n * GROUP, GROUP)], low.at[0], stage_sem.at[n]).wait()

        early = [(piece, chunk) for piece in range(EARLY) for chunk in range(n_chunks)]
        late = [(piece, chunk) for chunk in range(n_chunks) for piece in range(EARLY, n_pieces)]
        units = early + late
        far = [(piece, chunk) for piece, chunk in units if not is_kept(piece // 2, chunk)]

        def fetch(count):
            piece, chunk = far[count % len(far)]
            slot = count % STAGES
            away = low_hbm.at[chunk, piece // 2, pl.ds(piece % 2 * PIECE, PIECE)]
            return pltpu.make_async_copy(away, stage.at[pl.ds(slot * PIECE, PIECE)], stage_sem.at[slot])

        def product(call, fetched, last, hooks):
            for number, (piece, chunk) in enumerate(units):
                for hook in hooks.get(number, ()):
                    hook()
                if chunk == 0:
                    take_piece(call - 1, piece)
                rows = slice(piece * PIECE, (piece + 1) * PIECE)
                cols = slice(chunk * CHUNK, (chunk + 1) * CHUNK)
                acc = jnp.dot(vecs[:, rows], high[rows, cols], preferred_element_type=F32)
                if is_kept(piece // 2, chunk):
                    below = low[chunk, piece % 2 * PIECE:(piece % 2 + 1) * PIECE]
                else:
                    fetch(fetched).wait()
                    below = stage[fetched % STAGES * PIECE:(fetched % STAGES + 1) * PIECE]
                acc_low = jnp.dot(vecs[0:VECS, rows], below, preferred_element_type=F32)
                if not is_kept(piece // 2, chunk):
                    if not (last and fetched + STAGES >= 2 * len(far)):
                        fetch(fetched + STAGES).start()
                    fetched += 1
                if piece == 0:
                    acc_ref[chunk, 0:3 * VECS] = acc
                    acc_ref[chunk, 3 * VECS:] = acc_low
                else:
                    acc_ref[chunk, 0:3 * VECS] += acc
                    acc_ref[chunk, 3 * VECS:] += acc_low
                if piece == n_pieces - 1:
                    send_part(call, chunk, acc_ref[chunk])
            return fetched

        row_of = lax.broadcasted_iota(jnp.int32, (VECS, 128), 0)
        lane_of = lax.broadcasted_iota(jnp.int32, (VECS, 128), 1)

        def dots_local(phase, values):
            line = jnp.zeros((1, 128), F32)
            for n, value in enumerate(values):
                here = lane_of == row_of + n * VECS
                line = line + jnp.sum(jnp.where(here, value, 0.0), axis=0, keepdims=True)
            block = jnp.broadcast_to(line, (8, 128))
            dot_a[phase] = block
            dot_a_all[phase, my_col] = block
            start_all(to_cols, 4 + phase, dot_a.at[phase], dot_a_all.at[phase], cols_n, my_col)

        def dot(x, y):
            return jnp.sum(x * y, axis=1, keepdims=True)

        def dots_row(phase):
            @pl.loop(1, cols_n)
            def _(k):
                slot = lax.rem(my_col + k, cols_n)
                to_cols(4 + phase, dot_a.at[phase], dot_a_all.at[phase], 1, slot).wait_recv()
            total = dot_a_all[phase, 0]
            for slot in range(1, cols_n):
                total = total + dot_a_all[phase, slot]
            dot_b[phase] = total
            dot_b_all[phase, my_row] = total
            start_all(to_rows, 3 + phase, dot_b.at[phase], dot_b_all.at[phase], rows_n, my_row)

        def dots_whole(phase, count):
            @pl.loop(1, rows_n)
            def _(k):
                slot = lax.rem(my_row + k, rows_n)
                to_rows(3 + phase, dot_b.at[phase], dot_b_all.at[phase], 1, slot).wait_recv()
            total = dot_b_all[phase, 0]
            for slot in range(1, rows_n):
                total = total + dot_b_all[phase, slot]
            line = jnp.broadcast_to(total[0:1], (VECS, 128))
            return [
                jnp.sum(jnp.where(lane_of == row_of + n * VECS, line, 0.0), axis=1, keepdims=True)
                for n in range(count)
            ]

        def sent_before():
            sent_all(to_cols, 0, points_own, right_all, cols_n)
            sent_all(to_rows, 0, first_own, first_all, rows_n)
            for call in range(2):
                sent_parts(call)
                sent_all(to_rows, 1 + call, vec_own.at[call], vec_all.at[call], rows_n)
                sent_all(to_cols, 6 + call, vec_own.at[call], col_all.at[call], cols_n)
                for place in range(cols_n):
                    arrived(to_cols, 6 + call, vec_own.at[call], col_all.at[call], place, my_place)

        def sent_parts(call):
            @pl.loop(1, cols_n)
            def _(k):
                part_copy(call, lax.rem(my_col + k, cols_n), 0).wait_send()

        def hooks_after(call):
            found = {}
            for turn in range(n_chunks):
                done = len(early) + (turn + 1) * (n_pieces - EARLY)
                at = done + LAG - len(units)
                if call == 0:
                    at = LAG if turn == n_chunks - 1 else None
                if at is not None and at >= 0:
                    found.setdefault(at, []).append(lambda turn=turn: owner_step(call, turn))
            return found

        def hooks_within(call):
            found = {}
            for turn in range(n_chunks):
                done = len(early) + (turn + 1) * (n_pieces - EARLY)
                if done + LAG < len(units):
                    found.setdefault(done + LAG, []).append(lambda turn=turn: owner_step(call, turn))
            return found

        def merged(*tables):
            found = {}
            for table in tables:
                for at, hooks in table.items():
                    found.setdefault(at, []).extend(hooks)
            return found

        for count in range(STAGES):
            fetch(count).start()
        fetched = product(1, 0, False, merged(hooks_after(0), hooks_within(1), {20: [lambda: spread_cols(0)]}))
        fetched = product(2, fetched, True, merged(
            hooks_after(1),
            {
                12: [lambda: spread_cols(1)],
                14: [lambda: dots_local(0, [dot(vec_own[0], vec_own[0]), dot(vec_own[0], vec_own[1])])],
                24: [lambda: dots_row(0)],
                28: [sent_before],
            },
        ))
        res0, image0 = vec_own[0], vec_own[1]
        norm0, curve0 = dots_whole(0, 2)
        alpha0 = norm0 / curve0
        res1 = res0 - alpha0 * image0
        crossed = jnp.zeros((VECS, own), F32)
        for place in range(cols_n):
            owner = lax.rem(first_turn + place // pair, turns) * pair + place % pair
            there = col_all[0, place] - alpha0 * col_all[1, place]
            crossed = crossed + there * part[2, owner]
        dots_local(1, [dot(res1, res1), dot(res1, image0), jnp.sum(crossed, axis=1, keepdims=True)])
        dots_row(1)
        image1 = reduced(2, image0)
        half = image0 - alpha0 * image1
        norm1, cross, crossed = dots_whole(1, 3)
        own_curve = cross - alpha0 * (crossed + NOISE_VAR * cross)
        beta0 = norm1 / norm0
        curve1 = own_curve + 2.0 * beta0 * cross + beta0 * beta0 * curve0
        alpha1 = norm1 / curve1
        out_ref[0] = init_ref[...] + alpha0 * res0
        out_ref[1] = alpha1 * (res1 + beta0 * res0)
        out_ref[2] = res1
        out_ref[3] = -alpha1 * (half + beta0 * image0)
        sent_parts(2)
        for phase in range(2):
            sent_all(to_cols, 4 + phase, dot_a.at[phase], dot_a_all.at[phase], cols_n)
            sent_all(to_rows, 3 + phase, dot_b.at[phase], dot_b_all.at[phase], rows_n)

    def scratch():
        return [
            pltpu.VMEM((span, wide), BF16),
            pltpu.VMEM((n_chunks, GROUP, CHUNK), BF16),
            pltpu.VMEM((STAGES * PIECE, CHUNK), BF16),
            pltpu.VMEM((span, DEPTH), BF16),
            pltpu.VMEM((DEPTH, wide), BF16),
            pltpu.VMEM((3 * VECS, span), BF16),
            pltpu.VMEM((n_chunks, 4 * VECS, CHUNK), F32),
            pltpu.VMEM((2 * VECS, own), F32),
            pltpu.VMEM((rows_n, 2 * VECS, own), F32),
            pltpu.VMEM((cols_n, VECS, own), F32),
            pltpu.VMEM((2, VECS, own), F32),
            pltpu.VMEM((2, rows_n, VECS, own), F32),
            pltpu.VMEM((2, cols_n, VECS, own), F32),
            pltpu.VMEM((3, cols_n, VECS, own), F32),
            pltpu.VMEM((3, cols_n, VECS, own), F32),
            pltpu.VMEM((2, 8, 128), F32),
            pltpu.VMEM((2, cols_n, 8, 128), F32),
            pltpu.VMEM((2, 8, 128), F32),
            pltpu.VMEM((2, rows_n, 8, 128), F32),
            pltpu.SemaphoreType.DMA((8, cols_n)),
            pltpu.SemaphoreType.DMA((8, cols_n)),
            pltpu.SemaphoreType.DMA((5, rows_n)),
            pltpu.SemaphoreType.DMA((5, rows_n)),
            pltpu.SemaphoreType.DMA((STAGES,)),
        ]

    vmem = pl.BlockSpec(memory_space=pltpu.VMEM)
    return pl.pallas_call(
        kernel,
        out_shape=[
            jax.ShapeDtypeStruct((4, VECS, own), F32),
            jax.ShapeDtypeStruct((n_chunks, turns, GROUP, CHUNK), BF16),
        ],
        in_specs=[vmem] * 4,
        out_specs=[vmem, pl.BlockSpec(memory_space=pl.ANY)],
        scratch_shapes=scratch(),
        compiler_params=pltpu.CompilerParams(
            collective_id=0, has_side_effects=True, vmem_limit_bytes=63 * 2**20
        ),
        name="conjugate_gradients",
    )


def solution(mesh):
    rows_n, cols_n = mesh.shape["row"], mesh.shape["col"]

    def shards(points, targets, initial, lengthscale):
        call = make_kernel(rows_n, cols_n, points.shape[0])
        out, _ = call(points.T, initial.T, targets.T, lengthscale[None, :])
        return (out[0] + out[1]).T, (out[2] + out[3]).T

    spec = P(("row", "col"), None)
    return jax.shard_map(
        shards, mesh=mesh, in_specs=(spec, spec, spec, P()), out_specs=(spec, spec), check_vma=False
    )
```

```python
import math

import jax
import jax.numpy as jnp
from jax import lax
from jax.experimental import pallas as pl
from jax.experimental.pallas import tpu as pltpu
from jax.sharding import PartitionSpec as P

MESH = pl.DeviceIdType.MESH
F32, BF16 = jnp.float32, jnp.bfloat16
NOISE_VAR = 0.5
LN2 = math.log(2.0)
DIST_SCALE = math.sqrt(5.0) / LN2
VECS = 16
DEPTH = 128
CHUNK = 768
PIECE = 768
GROUP = 2 * PIECE
SUB = 768
TILE = 256
STAGES = 4
EARLY = 3
LAG = 6


def split3(x):
    first = x.astype(BF16)
    rest = x - first.astype(F32)
    second = rest.astype(BF16)
    third = (rest - second.astype(F32)).astype(BF16)
    return first, second, third


def stacked(z, left):
    a, b, c = split3(z)
    qa, qb, qc = split3(jnp.sum(z * z, axis=0, keepdims=True))
    row = lax.broadcasted_iota(jnp.int32, z.shape, 0)
    base = 0 if left else 3
    tail = jnp.where(row == base, qa.astype(F32), 0.0)
    tail = jnp.where(row == base + 1, qb.astype(F32), tail)
    tail = jnp.where(row == base + 2, qc.astype(F32), tail)
    other = 3 - base
    tail = jnp.where((row >= other) & (row < other + 3), 1.0, tail)
    a, b, c = a.astype(F32), b.astype(F32), c.astype(F32)
    zero = jnp.zeros_like(tail)
    if left:
        return jnp.concatenate([a, a, b, b, a, c, tail, zero], axis=0)
    a, b, c = -2.0 * a, -2.0 * b, -2.0 * c
    return jnp.concatenate([a, b, a, b, c, a, tail, zero], axis=0)


def matern(s):
    s = jnp.maximum(s, 1e-30)
    dist = s * lax.rsqrt(s)
    shifted = dist + 1.5 / LN2
    return (shifted * shifted + 0.75 / LN2**2) * jnp.exp2(math.log2(LN2**2 / 3.0) - dist)


def make_kernel(rows_n, cols_n, own):
    span = rows_n * own
    wide = cols_n * own
    n_chunks = wide // CHUNK
    n_pieces = span // PIECE
    pair = CHUNK // own
    turns = n_chunks
    each = rows_n // turns

    def is_kept(group, chunk):
        return (group + chunk) % turns == 0

    def kernel(
        pts_ref, init_ref, targ_ref, scale_ref,
        out_ref, low_hbm,
        high, low, stage, left, right, vecs, acc_ref, first_own, first_all, right_all,
        vec_own, vec_all, col_all, part, part_all, dot_a, dot_a_all, dot_b, dot_b_all,
        col_send, col_recv, row_send, row_recv, stage_sem,
    ):
        my_row, my_col = lax.axis_index("row"), lax.axis_index("col")
        first_turn = lax.rem(my_row, turns)
        my_turn = lax.rem(my_col // pair - first_turn + turns, turns)
        my_slot = my_turn * each + my_row // turns
        my_place = my_turn * pair + lax.rem(my_col, pair)

        barrier = pltpu.get_barrier_semaphore()

        @pl.loop(1, rows_n)
        def _(k):
            pl.semaphore_signal(
                barrier, inc=1, device_id=(lax.rem(my_row + k, rows_n), my_col), device_id_type=MESH
            )

        @pl.loop(1, cols_n)
        def _(k):
            pl.semaphore_signal(
                barrier, inc=1, device_id=(my_row, lax.rem(my_col + k, cols_n)), device_id_type=MESH
            )

        square = (VECS, VECS)
        on_diagonal = lax.broadcasted_iota(jnp.int32, square, 0) == lax.broadcasted_iota(jnp.int32, square, 1)
        scales = jnp.broadcast_to(scale_ref[...], square)
        scale = jnp.sum(jnp.where(on_diagonal, scales, 0.0), axis=1, keepdims=True)
        z_own = pts_ref[...] / scale * DIST_SCALE
        first_own[0:VECS, :] = z_own
        first_own[VECS:, :] = init_ref[...]
        pl.semaphore_wait(barrier, rows_n - 1 + cols_n - 1)

        def to_rows(phase, src, dst, k, slot):
            return pltpu.make_async_remote_copy(
                src_ref=src, dst_ref=dst.at[slot],
                send_sem=row_send.at[phase], recv_sem=row_recv.at[phase, slot],
                device_id=(lax.rem(my_row + k, rows_n), my_col), device_id_type=MESH,
            )

        def to_cols(phase, src, dst, k, slot):
            return pltpu.make_async_remote_copy(
                src_ref=src, dst_ref=dst.at[slot],
                send_sem=col_send.at[phase], recv_sem=col_recv.at[phase, slot],
                device_id=(my_row, lax.rem(my_col + k, cols_n)), device_id_type=MESH,
            )

        def start_all(make, phase, src, dst, count, slot):
            @pl.loop(1, count)
            def _(k):
                make(phase, src, dst, k, slot).start()

        def sent_all(sems, phase, dst, count):
            bulk = dst.at[pl.ds(0, count - 1)]
            pltpu.make_async_copy(bulk, bulk, sems.at[phase]).wait()

        def arrived(make, phase, src, dst, slot, mine):
            @pl.when(slot != mine)
            def _():
                make(phase, src, dst, 1, slot).wait_recv()

        points_own = first_own.at[pl.ds(0, VECS)]
        for n in range(1, each):
            to_rows(0, first_own, first_all, n * turns, my_slot).start()

        @pl.when(my_turn == 0)
        def _():
            start_all(to_cols, 0, points_own, right_all, cols_n, my_place)

        def send_group(turn):
            @pl.loop(0, each)
            def _(n):
                to_rows(0, first_own, first_all, n * turns + turn, my_slot).start()

        send_group(1)
        first_all[my_slot] = first_own[...]
        right_all[my_place] = z_own

        def put_vecs(slot, block):
            here = pl.ds(pl.multiple_of(slot * own, 128), own)
            a, b, c = split3(block)
            vecs[0:VECS, here] = a
            vecs[VECS:2 * VECS, here] = b
            vecs[2 * VECS:, here] = c

        def part_copy(call, owner, sender):
            k = lax.rem(owner - my_col + cols_n, cols_n)
            return to_cols(1 + call, part.at[call, owner], part_all.at[call], k, sender)

        def send_part(call, turn, acc):
            total = acc[0:VECS] + acc[VECS:2 * VECS] + acc[2 * VECS:3 * VECS] + acc[3 * VECS:]
            for n in range(pair):
                owner = lax.rem(first_turn + turn, turns) * pair + n
                part[call, owner] = total[:, n * own:(n + 1) * own]

                @pl.when(owner != my_col)
                def _():
                    part_copy(call, owner, my_col).start()

        def reduced(call, block):
            @pl.loop(1, cols_n)
            def _(k):
                part_copy(call, lax.rem(my_col + 1, cols_n), lax.rem(my_col + k, cols_n)).wait_recv()
            part_all[call, my_col] = part[call, my_col]
            total = part_all[call, 0]
            for slot in range(1, cols_n):
                total = total + part_all[call, slot]
            return total + NOISE_VAR * block

        def owner_step(call, turn):
            @pl.when(my_turn == turn)
            def _():
                if call == 0:
                    block = targ_ref[...] - reduced(0, init_ref[...])
                else:
                    block = reduced(1, vec_own[0])
                vec_own[call] = block
                vec_all[call, my_slot] = block
                start_all(to_rows, 1 + call, vec_own.at[call], vec_all.at[call], rows_n, my_slot)
                col_all[call, my_place] = block

        def spread_cols(call):
            start_all(to_cols, 6 + call, vec_own.at[call], col_all.at[call], cols_n, my_place)

        def take_piece(call, piece):
            for n in range(2):
                slot = piece * 2 + n
                arrived(to_rows, 1 + call, vec_own.at[call], vec_all.at[call], slot, my_slot)
                put_vecs(slot, vec_all[call, slot])

        @pl.loop(0, n_chunks)
        def _(chunk):
            for n in range(pair):
                place = chunk * pair + n
                arrived(to_cols, 0, points_own, right_all, place, my_place)
                right[:, pl.ds(pl.multiple_of(place * own, 128), own)] = stacked(right_all[place], False).astype(BF16)
            acc_ref[0] = jnp.zeros((4 * VECS, CHUNK), F32)

            @pl.loop(0, turns)
            def _(turn):
                group = lax.rem(my_turn + turn, turns)

                @pl.when(chunk == 0)
                def _():
                    for n in range(each):
                        slot = group * each + n
                        arrived(to_rows, 0, first_own, first_all, slot, my_slot)
                        here = pl.ds(pl.multiple_of(slot * own, 128), own)
                        left[here, :] = stacked(first_all[slot, 0:VECS], True).T.astype(BF16)
                        put_vecs(slot, first_all[slot, VECS:])

                    @pl.when(turn + 2 < turns)
                    def _():
                        send_group(turn + 2)

                    @pl.when((turn == 0) & (my_turn != 0))
                    def _():
                        start_all(to_cols, 0, points_own, right_all, cols_n, my_place)

                count = chunk * turns + turn
                half = pl.ds(pl.multiple_of(lax.rem(count, 2) * GROUP, GROUP), GROUP)
                sem = stage_sem.at[lax.rem(count, 2)]

                @pl.when(count >= 2)
                def _():
                    pltpu.make_async_copy(stage.at[half], low.at[0], sem).wait()

                for sub in range(GROUP // SUB):
                    rows = pl.ds(pl.multiple_of(group * GROUP + sub * SUB, SUB), SUB)
                    staged = pl.ds(pl.multiple_of(lax.rem(count, 2) * GROUP + sub * SUB, SUB), SUB)
                    for n in range(0, CHUNK, TILE):
                        here = pl.ds(pl.multiple_of(chunk * CHUNK + n, TILE), TILE)
                        m = matern(jnp.dot(left[rows, :], right[:, here], preferred_element_type=F32))
                        h = m.astype(BF16)
                        l = (m - h.astype(F32)).astype(BF16)
                        high[rows, here] = h
                        stage[staged, n:n + TILE] = l
                        acc_ref[0, 0:3 * VECS, n:n + TILE] += jnp.dot(vecs[:, rows], h, preferred_element_type=F32)
                        acc_ref[0, 3 * VECS:, n:n + TILE] += jnp.dot(vecs[0:VECS, rows], l, preferred_element_type=F32)

                kept = is_kept(group, chunk)

                @pl.when(kept)
                def _():
                    pltpu.make_async_copy(stage.at[half], low.at[chunk], sem).start()

                @pl.when(jnp.logical_not(kept))
                def _():
                    pltpu.make_async_copy(stage.at[half], low_hbm.at[chunk, group], sem).start()

            send_part(0, chunk, acc_ref[0])
            for turn in range(n_chunks - 1):
                @pl.when(chunk == turn + 1)
                def _():
                    owner_step(0, turn)

        for n in range(2):
            pltpu.make_async_copy(stage.at[pl.ds(n * GROUP, GROUP)], low.at[0], stage_sem.at[n]).wait()

        early = [(piece, chunk) for piece in range(EARLY) for chunk in range(n_chunks)]
        late = [(piece, chunk) for chunk in range(n_chunks) for piece in range(EARLY, n_pieces)]
        units = early + late
        far = [(piece, chunk) for piece, chunk in units if not is_kept(piece // 2, chunk)]

        def fetch(count):
            piece, chunk = far[count % len(far)]
            slot = count % STAGES
            away = low_hbm.at[chunk, piece // 2, pl.ds(piece % 2 * PIECE, PIECE)]
            return pltpu.make_async_copy(away, stage.at[pl.ds(slot * PIECE, PIECE)], stage_sem.at[slot])

        def product(call, fetched, last, hooks):
            for number, (piece, chunk) in enumerate(units):
                for hook in hooks.get(number, ()):
                    hook()
                if chunk == 0:
                    take_piece(call - 1, piece)
                rows = slice(piece * PIECE, (piece + 1) * PIECE)
                cols = slice(chunk * CHUNK, (chunk + 1) * CHUNK)
                acc = jnp.dot(vecs[:, rows], high[rows, cols], preferred_element_type=F32)
                if is_kept(piece // 2, chunk):
                    below = low[chunk, piece % 2 * PIECE:(piece % 2 + 1) * PIECE]
                else:
                    fetch(fetched).wait()
                    below = stage[fetched % STAGES * PIECE:(fetched % STAGES + 1) * PIECE]
                acc_low = jnp.dot(vecs[0:VECS, rows], below, preferred_element_type=F32)
                if not is_kept(piece // 2, chunk):
                    if not (last and fetched + STAGES >= 2 * len(far)):
                        fetch(fetched + STAGES).start()
                    fetched += 1
                if piece == 0:
                    acc_ref[chunk, 0:3 * VECS] = acc
                    acc_ref[chunk, 3 * VECS:] = acc_low
                else:
                    acc_ref[chunk, 0:3 * VECS] += acc
                    acc_ref[chunk, 3 * VECS:] += acc_low
                if piece == n_pieces - 1:
                    send_part(call, chunk, acc_ref[chunk])
            return fetched

        row_of = lax.broadcasted_iota(jnp.int32, (VECS, 128), 0)
        lane_of = lax.broadcasted_iota(jnp.int32, (VECS, 128), 1)

        def dots_local(phase, values):
            line = jnp.zeros((1, 128), F32)
            for n, value in enumerate(values):
                here = lane_of == row_of + n * VECS
                line = line + jnp.sum(jnp.where(here, value, 0.0), axis=0, keepdims=True)
            dot_a[phase] = line
            dot_a_all[phase, my_col] = line
            start_all(to_cols, 4 + phase, dot_a.at[phase], dot_a_all.at[phase], cols_n, my_col)

        def dot(x, y):
            return jnp.sum(x * y, axis=1, keepdims=True)

        def dots_row(phase):
            @pl.loop(1, cols_n)
            def _(k):
                slot = lax.rem(my_col + k, cols_n)
                to_cols(4 + phase, dot_a.at[phase], dot_a_all.at[phase], 1, slot).wait_recv()
            total = dot_a_all[phase, 0]
            for slot in range(1, cols_n):
                total = total + dot_a_all[phase, slot]
            dot_b[phase] = total
            dot_b_all[phase, my_row] = total
            start_all(to_rows, 3 + phase, dot_b.at[phase], dot_b_all.at[phase], rows_n, my_row)

        def dots_whole(phase, count):
            @pl.loop(1, rows_n)
            def _(k):
                slot = lax.rem(my_row + k, rows_n)
                to_rows(3 + phase, dot_b.at[phase], dot_b_all.at[phase], 1, slot).wait_recv()
            total = dot_b_all[phase, 0]
            for slot in range(1, rows_n):
                total = total + dot_b_all[phase, slot]
            line = jnp.broadcast_to(total, (VECS, 128))
            return [
                jnp.sum(jnp.where(lane_of == row_of + n * VECS, line, 0.0), axis=1, keepdims=True)
                for n in range(count)
            ]

        def sent_before():
            sent_all(col_send, 0, right_all, cols_n)
            sent_all(row_send, 0, first_all, rows_n)
            for call in range(2):
                sent_parts(call)
                sent_all(row_send, 1 + call, vec_all.at[call], rows_n)
                sent_all(col_send, 6 + call, col_all.at[call], cols_n)
                for place in range(cols_n):
                    arrived(to_cols, 6 + call, vec_own.at[call], col_all.at[call], place, my_place)

        def sent_parts(call):
            sent_all(col_send, 1 + call, part_all.at[call], cols_n)

        def hooks_after(call):
            found = {}
            for turn in range(n_chunks):
                done = len(early) + (turn + 1) * (n_pieces - EARLY)
                at = done + LAG - len(units)
                if call == 0:
                    at = LAG if turn == n_chunks - 1 else None
                if at is not None and at >= 0:
                    found.setdefault(at, []).append(lambda turn=turn: owner_step(call, turn))
            return found

        def hooks_within(call):
            found = {}
            for turn in range(n_chunks):
                done = len(early) + (turn + 1) * (n_pieces - EARLY)
                if done + LAG < len(units):
                    found.setdefault(done + LAG, []).append(lambda turn=turn: owner_step(call, turn))
            return found

        def merged(*tables):
            found = {}
            for table in tables:
                for at, hooks in table.items():
                    found.setdefault(at, []).extend(hooks)
            return found

        for count in range(STAGES):
            fetch(count).start()
        fetched = product(1, 0, False, merged(hooks_after(0), hooks_within(1), {20: [lambda: spread_cols(0)]}))
        fetched = product(2, fetched, True, merged(
            hooks_after(1),
            {
                12: [lambda: spread_cols(1)],
                14: [lambda: dots_local(0, [dot(vec_own[0], vec_own[0]), dot(vec_own[0], vec_own[1])])],
                24: [lambda: dots_row(0)],
                28: [sent_before],
            },
        ))
        res0, image0 = vec_own[0], vec_own[1]
        norm0, curve0 = dots_whole(0, 2)
        alpha0 = norm0 / curve0
        res1 = res0 - alpha0 * image0
        crossed = jnp.zeros((VECS, own), F32)
        for place in range(cols_n):
            owner = lax.rem(first_turn + place // pair, turns) * pair + place % pair
            there = col_all[0, place] - alpha0 * col_all[1, place]
            crossed = crossed + there * part[2, owner]
        dots_local(1, [dot(res1, res1), dot(res1, image0), jnp.sum(crossed, axis=1, keepdims=True)])
        dots_row(1)
        image1 = reduced(2, image0)
        half = image0 - alpha0 * image1
        norm1, cross, crossed = dots_whole(1, 3)
        own_curve = cross - alpha0 * (crossed + NOISE_VAR * cross)
        beta0 = norm1 / norm0
        curve1 = own_curve + 2.0 * beta0 * cross + beta0 * beta0 * curve0
        alpha1 = norm1 / curve1
        out_ref[0] = init_ref[...] + alpha0 * res0
        out_ref[1] = alpha1 * (res1 + beta0 * res0)
        out_ref[2] = res1
        out_ref[3] = -alpha1 * (half + beta0 * image0)
        sent_parts(2)
        for phase in range(2):
            sent_all(col_send, 4 + phase, dot_a_all.at[phase], cols_n)
            sent_all(row_send, 3 + phase, dot_b_all.at[phase], rows_n)

    def scratch():
        return [
            pltpu.VMEM((span, wide), BF16),
            pltpu.VMEM((n_chunks, GROUP, CHUNK), BF16),
            pltpu.VMEM((STAGES * PIECE, CHUNK), BF16),
            pltpu.VMEM((span, DEPTH), BF16),
            pltpu.VMEM((DEPTH, wide), BF16),
            pltpu.VMEM((3 * VECS, span), BF16),
            pltpu.VMEM((n_chunks, 4 * VECS, CHUNK), F32),
            pltpu.VMEM((2 * VECS, own), F32),
            pltpu.VMEM((rows_n, 2 * VECS, own), F32),
            pltpu.VMEM((cols_n, VECS, own), F32),
            pltpu.VMEM((2, VECS, own), F32),
            pltpu.VMEM((2, rows_n, VECS, own), F32),
            pltpu.VMEM((2, cols_n, VECS, own), F32),
            pltpu.VMEM((3, cols_n, VECS, own), F32),
            pltpu.VMEM((3, cols_n, VECS, own), F32),
            pltpu.VMEM((2, 1, 128), F32),
            pltpu.VMEM((2, cols_n, 1, 128), F32),
            pltpu.VMEM((2, 1, 128), F32),
            pltpu.VMEM((2, rows_n, 1, 128), F32),
            pltpu.SemaphoreType.DMA((8,)),
            pltpu.SemaphoreType.DMA((8, cols_n)),
            pltpu.SemaphoreType.DMA((5,)),
            pltpu.SemaphoreType.DMA((5, rows_n)),
            pltpu.SemaphoreType.DMA((STAGES,)),
        ]

    vmem = pl.BlockSpec(memory_space=pltpu.VMEM)
    return pl.pallas_call(
        kernel,
        out_shape=[
            jax.ShapeDtypeStruct((4, VECS, own), F32),
            jax.ShapeDtypeStruct((n_chunks, turns, GROUP, CHUNK), BF16),
        ],
        in_specs=[vmem] * 4,
        out_specs=[vmem, pl.BlockSpec(memory_space=pl.ANY)],
        scratch_shapes=scratch(),
        compiler_params=pltpu.CompilerParams(
            collective_id=0, has_side_effects=True, vmem_limit_bytes=63 * 2**20
        ),
        name="conjugate_gradients",
    )


def solution(mesh):
    rows_n, cols_n = mesh.shape["row"], mesh.shape["col"]

    def shards(points, targets, initial, lengthscale):
        call = make_kernel(rows_n, cols_n, points.shape[0])
        out, _ = call(points.T, initial.T, targets.T, lengthscale[None, :])
        return (out[0] + out[1]).T, (out[2] + out[3]).T

    spec = P(("row", "col"), None)
    return jax.shard_map(
        shards, mesh=mesh, in_specs=(spec, spec, spec, P()), out_specs=(spec, spec), check_vma=False
    )
```
